128 devices in a mesh: dp: 4 (over y_hi, core), row: 8 (over x, y_lo), col: 4 (over z).
Axes of the slice: x: 4, y: 4 (y_hi: 2, y_lo: 2; y = y_hi * 2 + y_lo), z: 4, core: 2. Of those that a mesh axis runs over, the one named last changes fastest.
Arguments:
- inputs: bfloat16 [2, 8192, 4096], P(None, ('dp', 'col'), 'row'), may hold values from -6 to 6
- out_grads: bfloat16 [4, 8192, 4096], P(None, ('dp', 'row'), 'col'), may hold values from -0.06629126 to 0.06629126
- weights: float32 [4, 4096, 4096], P(None, 'row', 'col'), may hold values from -2 to 2
- row_moment: float32 [4, 4096], P(None, 'row'), may hold values from 0.01 to 1
- col_moment: float32 [4, 4096], P(None, 'col'), may hold values from 0.1 to 1
Outputs:
- weight_change: float32 [4, 4096, 4096], P(None, 'row', 'col')
- new_row: float32 [4, 4096], P(None, 'row')
- new_col: float32 [4, 4096], P(None, 'col')
The draws below stay inside these ranges and needn't reach their ends.
All inputs are finite; a program needn't handle non-finite values.
Results may differ from the reference program's by a relative error of at most 0.0003.
Values may be sent and summed in bfloat16 or wider, within the bound.
A program may use at most 128 MiB of HBM per device.

```python
import math
import jax
import jax.numpy as jnp
from jax import lax

D = 4096
STEP = 10
TOKENS = 8192


def draw_inputs(key, part):
    key = jax.random.fold_in(key, 5)
    keys = jax.random.split(key, 4)
    noise = jax.random.normal(keys[0], (2, TOKENS, D), jnp.float32)
    lowest = math.log(0.3)
    highest = math.log(3.0)
    token_signs = jnp.where(jax.random.bernoulli(keys[1], 0.5, (2, TOKENS)), 1.0, -1.0)
    pattern_signs = jnp.where(jax.random.bernoulli(keys[2], 0.5, (2, D)), 1.0, -1.0)
    pattern = jnp.exp(jax.random.uniform(keys[3], (2, D), jnp.float32, lowest, highest)) * pattern_signs
    values = noise + token_signs[:, :, None] * pattern[:, None, :]
    return jnp.clip(values, -6.0, 6.0).astype(jnp.bfloat16)


def draw_weights(key, part):
    key = jax.random.fold_in(key, 11)
    keys = jax.random.split(key, 6)
    noise = jax.random.normal(keys[0], (4, D, D), jnp.float32)
    top = math.log(10.0)
    rising = jnp.arange(D, dtype=jnp.float32) / float(D - 1) * (0.5 * math.log(3.0))
    row_scale = jnp.exp(jax.random.uniform(keys[1], (4, D), jnp.float32, 0.0, top) + rising[None, :])
    col_scale = jnp.exp(jax.random.uniform(keys[2], (4, D), jnp.float32, 0.0, top) + rising[None, :])
    levels = jnp.exp(jax.random.uniform(keys[3], (4,), jnp.float32, math.log(5.5e-05), math.log(0.00083)))
    lowest = jnp.exp(jax.random.uniform(keys[4], (), jnp.float32, math.log(5.5e-06), math.log(1.4e-05)))
    chosen = jax.random.randint(keys[5], (), 0, 4)
    levels = jnp.where(jnp.arange(4) == chosen, lowest, levels)
    return noise * levels[:, None, None] * row_scale[:, :, None] * col_scale[:, None, :]


def draw_out_grads(key, part):
    key = jax.random.fold_in(key, 23)
    noise = jnp.clip(jax.random.normal(key, (4, TOKENS, D), jnp.float32), -6.0, 6.0)
    factors = jnp.array([1.0, 1.0, 0.05, 0.05], jnp.float32) * float(TOKENS) ** (-0.5)
    return (noise * factors[:, None, None]).astype(jnp.bfloat16)


def draw_row_moment(key, part):
    key = jax.random.fold_in(key, 37)
    position = jnp.arange(D, dtype=jnp.float32) / float(D - 1) - 1.0
    rising = jnp.exp(math.log(5.0) * position)
    noise = jnp.exp(jax.random.uniform(key, (4, D), jnp.float32, math.log(0.1), 0.0))
    return noise * rising[None, :]


def block_scale(rng, extent, pieces, smallest, largest):
    def one(dim, parts):
        steps = jax.random.uniform(jax.random.fold_in(jax.random.fold_in(rng, 6), dim), (parts,), jnp.float32, smallest / len(pieces), largest / len(pieces))
        return jnp.repeat(jnp.exp(steps), extent[dim] // parts).reshape((-1,) + (1,) * (len(extent) - dim - 1))

    level = one(*pieces[0])
    for cut in pieces[1:]:
        level = level * one(*cut)
    return level


def setup_inputs(seed: int = 0) -> dict:
    streams_of = jax.random.split(jax.random.key(seed), 6)
    return {
        "inputs": draw_inputs(jax.random.fold_in(streams_of[5], 71), 0),
        "out_grads": draw_out_grads(jax.random.fold_in(streams_of[5], 71), 0),
        "weights": draw_weights(jax.random.fold_in(streams_of[5], 71), 0),
        "row_moment": draw_row_moment(jax.random.fold_in(streams_of[5], 71), 0),
        "col_moment": jnp.clip(jnp.exp(math.log(1.0) - 2.3025851 * jax.random.uniform(streams_of[4], (4, D), jnp.float32) ** block_scale(streams_of[4], (4, D), ((1, 4),), -0.2, 0.2)), 0.1, 1.0),
    }


def reference(inputs, out_grads, weights, row_moment, col_moment):
    decay_rate = 1.0 - float(STEP) ** (-0.8)
    relative = min(0.01, float(STEP) ** (-0.5))
    changes = []
    new_rows = []
    new_cols = []
    for matrix in range(4):
        source = inputs[0] if matrix < 3 else inputs[1]
        gradient = jnp.dot(source.T, out_grads[matrix], preferred_element_type=jnp.float32)
        squares = gradient * gradient + 1e-30
        row_new = decay_rate * row_moment[matrix] + (1.0 - decay_rate) * (lax.optimization_barrier(jnp.sum(squares, 1)) / D)
        col_new = decay_rate * col_moment[matrix] + (1.0 - decay_rate) * (lax.optimization_barrier(jnp.sum(squares, 0)) / D)
        mean_row = jnp.sum(row_new) / D
        update = gradient * lax.rsqrt(row_new[:, None] * col_new[None, :] / mean_row)
        clip_factor = jnp.maximum(1.0, jnp.sqrt(jnp.sum(update * update) / (D * D)))
        params = weights[matrix]
        step_size = relative * jnp.maximum(0.001, jnp.sqrt(jnp.sum(params * params) / (D * D)))
        changes.append(-(step_size / clip_factor) * update)
        new_rows.append(row_new)
        new_cols.append(col_new)
    return (jnp.stack(changes), jnp.stack(new_rows), jnp.stack(new_cols))
```

```python
import jax
import jax.numpy as jnp
from jax import lax
from jax.experimental import pallas as pl
from jax.experimental.pallas import tpu as pltpu
from jax.sharding import PartitionSpec as P

D = 4096
STEP = 10
MESH = pl.DeviceIdType.MESH
TOK = 256
HALF = 512


def gradient_kernel(
    inputs, out_grads, out, lbuf, rbuf, part, core_in, pair_in, final,
    s_loc, s_ly, r_ly, s_ry, r_ry, s_xa, r_xa, s_xb, r_xb, s_xf, r_xf,
    s_z, r_z, s_zf, r_zf, s_core, r_core, s_pair, r_pair, s_gc, r_gc, s_gy, r_gy, s_gf, r_gf, s_out,
):
    dp, row, z = lax.axis_index("dp"), lax.axis_index("row"), lax.axis_index("col")
    yh, c, x, yl = dp // 2, dp % 2, row // 2, row % 2

    def device(dx=0, m=0, dz=0, other=False):
        h = 1 - yh if m & 2 else yh
        l = 1 - yl if m & 1 else yl
        return {
            "dp": h * 2 + (1 - c if other else c),
            "row": ((x + dx) % 4) * 2 + l,
            "col": (z + dz) % 4,
        }

    def send(src, dst, ss, rs, to):
        copy = pltpu.make_async_remote_copy(
            src_ref=src, dst_ref=dst, send_sem=ss, recv_sem=rs, device_id=to, device_id_type=MESH
        )
        copy.start()
        sent.append(copy)
        return copy

    sent = []
    neighbours = [device(dx=1), device(dx=-1), device(dz=1), device(dz=-1),
                  device(m=1), device(m=2), device(m=3), device(other=True)]
    barrier = pltpu.get_barrier_semaphore()
    for other in neighbours:
        pl.semaphore_signal(barrier, inc=1, device_id=other, device_id_type=MESH)
    pl.semaphore_wait(barrier, len(neighbours))

    def flip(bit, value):
        return 1 - value if bit else value

    def token_rows(m):
        h = yl
        if (m >> 1) ^ (m & 1):
            h = 1 - yl
        return pl.ds(pl.multiple_of(h * TOK, TOK), TOK)

    def columns(h):
        return pl.ds(pl.multiple_of(h * HALF, HALF), HALF)

    def l_part(s, m, dz=0):
        return lbuf.at[s, flip(m & 1, yl), (z + dz) % 4, flip(m & 2, yh)]

    def r_part(p, m, dx=0):
        return rbuf.at[p, (x + dx) % 4, flip(m, yh)]

    local = []
    for s in range(2):
        copy = pltpu.make_async_copy(inputs.at[s, token_rows(0), :], l_part(s, 0), s_loc.at[s])
        copy.start()
        local.append(copy)
    for p in range(4):
        copy = pltpu.make_async_copy(out_grads.at[p, :, columns(yh)], r_part(p, 0), s_loc.at[2 + p])
        copy.start()
        local.append(copy)

    ly, ry, xa, xb, xf, zz, zf = {}, {}, {}, {}, {}, {}, {}

    def send_ly(s, m):
        ly[s, m] = send(inputs.at[s, token_rows(m), :], l_part(s, 0), s_ly.at[s, m - 1], r_ly.at[s, m - 1], device(m=m))

    def send_ry(p):
        ry[p] = send(out_grads.at[p, :, columns(1 - yh)], r_part(p, 0), s_ry.at[p], r_ry.at[p], device(m=3))

    def send_xa(p):
        for d in range(2):
            xa[p, d] = send(out_grads.at[p, :, columns(yh)], r_part(p, 0), s_xa.at[p, d], r_xa.at[p, d], device(dx=1 - 2 * d))

    def send_xb(p):
        ry[p].wait_recv()
        for d in range(2):
            xb[p, d] = send(r_part(p, 1), r_part(p, 1), s_xb.at[p, d], r_xb.at[p, d], device(dx=1 - 2 * d))

    def send_xf(p):
        xa[p, 0].wait_recv()
        xf[p, 0] = send(r_part(p, 0, -1), r_part(p, 0, -1), s_xf.at[p, 0], r_xf.at[p, 0], device(dx=1))
        xb[p, 1].wait_recv()
        xf[p, 1] = send(r_part(p, 1, 1), r_part(p, 1, 1), s_xf.at[p, 1], r_xf.at[p, 1], device(dx=-1))

    def send_z(s, m):
        if m:
            ly[s, m].wait_recv()
        for d in range(2):
            src = l_part(s, m) if m else inputs.at[s, token_rows(0), :]
            zz[s, m, d] = send(src, l_part(s, m), s_z.at[s, m, d], r_z.at[s, m, d], device(dz=1 - 2 * d))

    def send_zf(s, m):
        d = m // 2
        back = 2 * d - 1
        zz[s, m, d].wait_recv()
        zf[s, m] = send(l_part(s, m, back), l_part(s, m, back), s_zf.at[s, m], r_zf.at[s, m], device(dz=-back))

    core, pair, to_core, to_y, fwd, outs = {}, {}, {}, {}, {}, []
    mine = pl.ds(pl.multiple_of(c * TOK, TOK), TOK)
    theirs = pl.ds(pl.multiple_of((1 - c) * TOK, TOK), TOK)

    def wait_r(p):
        local[2 + p].wait()
        for d in range(2):
            if d == 1:
                xa[p, d].wait_recv()
            else:
                xb[p, d].wait_recv()
            xf[p, d].wait_recv()

    def wait_l(s):
        local[s].wait()
        for m in range(4):
            zz[s, m, 1 - m // 2].wait_recv()
            zf[s, m].wait_recv()

    def compute(p):
        s = 0 if p < 3 else 1
        for l in range(2):
            right = rbuf[p].reshape(8 * TOK, HALF)

            def rows(rs):
                left = lbuf[s, l, :, :, :, rs].reshape(8 * TOK, TOK)
                part[p, l, rs, :] = lax.dot_general(
                    left, right, (((0,), (0,)), ((), ())), preferred_element_type=jnp.float32
                )

            rows(theirs)
            core[p, l] = send(
                part.at[p, l, theirs, :], core_in.at[p, l], s_core.at[p, l], r_core.at[p, l], device(other=True)
            )
            rows(mine)

    def reduce_cores(p):
        for l in range(2):
            core[p, l].wait_recv()
            part[p, l, mine, :] += core_in[p, l]
        pair[p] = send(part.at[p, 1 - yl, mine, :], pair_in.at[p], s_pair.at[p], r_pair.at[p], device(m=1))

    def finish(p):
        pair[p].wait_recv()
        final[p] = part[p, yl, mine, :] + pair_in[p]
        here = out.at[p, mine, columns(yh)]
        to_y[p] = send(final.at[p], here, s_gy.at[p], r_gy.at[p], device(m=2))
        to_core[p] = send(final.at[p], here, s_gc.at[p], r_gc.at[p], device(other=True))
        copy = pltpu.make_async_copy(final.at[p], here, s_out.at[p])
        copy.start()
        outs.append(copy)

    def forward(p):
        to_y[p].wait_recv()
        there = out.at[p, mine, columns(1 - yh)]
        fwd[p] = send(there, there, s_gf.at[p], r_gf.at[p], device(other=True))

    send_ry(0)
    for m in (1, 3, 2):
        send_ly(0, m)
    send_xa(0)
    send_z(0, 0)
    send_ry(1)
    send_z(1, 0)
    for m in (1, 3, 2):
        send_ly(1, m)
    send_ry(2)
    send_ry(3)
    send_xb(0)
    send_xa(1)
    for m in (1, 3, 2):
        send_z(0, m)
    send_xf(0)
    send_xb(1)
    send_xa(2)
    for m in (0, 1, 3, 2):
        send_zf(0, m)
    send_xf(1)
    send_xb(2)
    send_xa(3)
    for m in (1, 3, 2):
        send_z(1, m)
    wait_l(0)
    wait_r(0)
    compute(0)
    wait_r(1)
    compute(1)
    reduce_cores(0)
    reduce_cores(1)
    send_xf(2)
    send_xb(3)
    for m in (0, 1, 3, 2):
        send_zf(1, m)
    finish(0)
    wait_r(2)
    compute(2)
    send_xf(3)
    reduce_cores(2)
    finish(1)
    wait_l(1)
    wait_r(3)
    compute(3)
    reduce_cores(3)
    forward(0)
    finish(2)
    forward(1)
    finish(3)
    forward(2)
    forward(3)
    for p in range(4):
        to_core[p].wait_recv()
        fwd[p].wait_recv()
        outs[p].wait()
    for copy in sent:
        copy.wait_send()


def gradients(inputs, out_grads):
    dma = pltpu.SemaphoreType.DMA
    any_space = pl.BlockSpec(memory_space=pl.ANY)
    return pl.pallas_call(
        gradient_kernel,
        out_shape=jax.ShapeDtypeStruct((4, 512, 1024), jnp.float32),
        in_specs=[any_space, any_space],
        out_specs=any_space,
        scratch_shapes=[
            pltpu.VMEM((2, 2, 4, 2, TOK, HALF), jnp.bfloat16),
            pltpu.VMEM((4, 4, 2, TOK, HALF), jnp.bfloat16),
            pltpu.VMEM((4, 2, 512, HALF), jnp.float32),
            pltpu.VMEM((4, 2, TOK, HALF), jnp.float32),
            pltpu.VMEM((4, TOK, HALF), jnp.float32),
            pltpu.VMEM((4, TOK, HALF), jnp.float32),
            dma((6,)),
            dma((2, 3)), dma((2, 3)), dma((4,)), dma((4,)),
            dma((4, 2)), dma((4, 2)), dma((4, 2)), dma((4, 2)), dma((4, 2)), dma((4, 2)),
            dma((2, 4, 2)), dma((2, 4, 2)), dma((2, 4)), dma((2, 4)),
            dma((4, 2)), dma((4, 2)), dma((4,)), dma((4,)),
            dma((4,)), dma((4,)), dma((4,)), dma((4,)), dma((4,)), dma((4,)), dma((4,)),
        ],
        name="gradients",
        compiler_params=pltpu.CompilerParams(
            collective_id=0, has_side_effects=True, vmem_limit_bytes=56 * 2**20
        ),
    )(inputs, out_grads)


def local(inputs, out_grads, weights, row_moment, col_moment):
    decay_rate = 1.0 - float(STEP) ** (-0.8)
    relative = min(0.01, float(STEP) ** (-0.5))
    gradient = gradients(inputs, out_grads)
    squares = gradient * gradient + 1e-30
    row_part = jnp.sum(squares, 2)
    col_part = jnp.sum(squares, 1)
    param_part = jnp.sum(weights * weights, (1, 2))
    row_sums = lax.psum(row_part, "col")
    row_new = decay_rate * row_moment + (1.0 - decay_rate) * (row_sums / D)
    col_sums = lax.psum(col_part, "row")
    row_total = lax.psum(jnp.sum(row_new, 1), "row")
    param_total = lax.psum(param_part, ("row", "col"))
    col_new = decay_rate * col_moment + (1.0 - decay_rate) * (col_sums / D)
    mean_row = row_total / D
    update = gradient * lax.rsqrt(
        row_new[:, :, None] * col_new[:, None, :] / mean_row[:, None, None]
    )
    update_part = jnp.sum(update * update, (1, 2))
    update_total = lax.psum(update_part, ("row", "col"))
    clip_factor = jnp.maximum(1.0, jnp.sqrt(update_total / (D * D)))
    step_size = relative * jnp.maximum(0.001, jnp.sqrt(param_total / (D * D)))
    change = -(step_size / clip_factor)[:, None, None] * update
    return (change, row_new, col_new)


def solution(mesh):
    return jax.shard_map(
        local,
        mesh=mesh,
        in_specs=(
            P(None, ("dp", "col"), "row"),
            P(None, ("dp", "row"), "col"),
            P(None, "row", "col"),
            P(None, "row"),
            P(None, "col"),
        ),
        out_specs=(P(None, "row", "col"), P(None, "row"), P(None, "col")),
        check_vma=False,
    )
```

```python
import jax
import jax.numpy as jnp
from jax import lax
from jax.experimental import pallas as pl
from jax.experimental.pallas import tpu as pltpu
from jax.sharding import PartitionSpec as P

D = 4096
STEP = 10
MESH = pl.DeviceIdType.MESH
TOK = 256
HALF = 512


def gradient_kernel(
    inputs, out_grads, weights, row_moment, col_moment, out, out_row, out_col, out_left, out_right,
    lbuf, rbuf, part, core_in, pair_in, final, share, rowx, colx, rown, coln, sum1, sum2,
    s_loc, s_ly, r_ly, s_ry, r_ry, s_xa, r_xa, s_xb, r_xb, s_xf, r_xf,
    s_z, r_z, s_zf, r_zf, s_core, r_core, s_pair, r_pair, s_gc, r_gc, s_gy, r_gy, s_gf, r_gf, s_out,
    s_share, s_rx, r_rx, s_cx, r_cx, s_rn, r_rn, s_cn, r_cn, s_s1, r_s1, s_s2, r_s2,
):
    dp, row, z = lax.axis_index("dp"), lax.axis_index("row"), lax.axis_index("col")
    yh, c, x, yl = dp // 2, dp % 2, row // 2, row % 2

    def device(dx=0, m=0, dz=0, other=False):
        h = 1 - yh if m & 2 else yh
        l = 1 - yl if m & 1 else yl
        return {
            "dp": h * 2 + (1 - c if other else c),
            "row": ((x + dx) % 4) * 2 + l,
            "col": (z + dz) % 4,
        }

    def send(src, dst, ss, rs, to):
        copy = pltpu.make_async_remote_copy(
            src_ref=src, dst_ref=dst, send_sem=ss, recv_sem=rs, device_id=to, device_id_type=MESH
        )
        copy.start()
        sent.append(copy)
        return copy

    sent = []
    row_peers = [(dz * 2 + h, device(dz=dz, m=2 * h)) for dz in range(4) for h in range(2) if dz + h]
    col_peers = [
        (dx * 4 + l * 2 + o, device(dx=dx, m=l, other=bool(o)))
        for dx in range(4) for l in range(2) for o in range(2) if dx + l + o
    ]
    neighbours = [to for _, to in row_peers + col_peers] + [device(m=3)]
    barrier = pltpu.get_barrier_semaphore()
    for other in neighbours:
        pl.semaphore_signal(barrier, inc=1, device_id=other, device_id_type=MESH)
    pl.semaphore_wait(barrier, len(neighbours))

    def flip(bit, value):
        return 1 - value if bit else value

    def token_rows(m):
        h = yl
        if (m >> 1) ^ (m & 1):
            h = 1 - yl
        return pl.ds(pl.multiple_of(h * TOK, TOK), TOK)

    def columns(h):
        return pl.ds(pl.multiple_of(h * HALF, HALF), HALF)

    def l_part(s, m, dz=0):
        return lbuf.at[s, flip(m & 1, yl), (z + dz) % 4, flip(m & 2, yh)]

    def r_part(p, m, dx=0):
        return rbuf.at[p, (x + dx) % 4, flip(m, yh)]

    quarter = pl.ds(pl.multiple_of(dp * 128, 128), 128)
    own_weights = pltpu.make_async_copy(weights.at[:, quarter, :], share, s_share.at[0])
    local = []
    for s in range(2):
        copy = pltpu.make_async_copy(inputs.at[s, token_rows(0), :], l_part(s, 0), s_loc.at[s])
        copy.start()
        local.append(copy)
    for p in range(4):
        copy = pltpu.make_async_copy(out_grads.at[p, :, columns(yh)], r_part(p, 0), s_loc.at[2 + p])
        copy.start()
        local.append(copy)

    ly, ry, xa, xb, xf, zz, zf = {}, {}, {}, {}, {}, {}, {}

    def send_ly(s, m):
        ly[s, m] = send(inputs.at[s, token_rows(m), :], l_part(s, 0), s_ly.at[s, m - 1], r_ly.at[s, m - 1], device(m=m))

    def send_ry(p):
        ry[p] = send(out_grads.at[p, :, columns(1 - yh)], r_part(p, 0), s_ry.at[p], r_ry.at[p], device(m=3))

    def send_xa(p):
        for d in range(2):
            xa[p, d] = send(out_grads.at[p, :, columns(yh)], r_part(p, 0), s_xa.at[p, d], r_xa.at[p, d], device(dx=1 - 2 * d))

    def send_xb(p):
        ry[p].wait_recv()
        for d in range(2):
            xb[p, d] = send(r_part(p, 1), r_part(p, 1), s_xb.at[p, d], r_xb.at[p, d], device(dx=1 - 2 * d))

    def send_xf(p):
        xa[p, 0].wait_recv()
        xf[p, 0] = send(r_part(p, 0, -1), r_part(p, 0, -1), s_xf.at[p, 0], r_xf.at[p, 0], device(dx=1))
        xb[p, 1].wait_recv()
        xf[p, 1] = send(r_part(p, 1, 1), r_part(p, 1, 1), s_xf.at[p, 1], r_xf.at[p, 1], device(dx=-1))

    def send_z(s, m):
        if m:
            ly[s, m].wait_recv()
        for d in range(2):
            src = l_part(s, m) if m else inputs.at[s, token_rows(0), :]
            zz[s, m, d] = send(src, l_part(s, m), s_z.at[s, m, d], r_z.at[s, m, d], device(dz=1 - 2 * d))

    def send_zf(s, m):
        d = m // 2
        back = 2 * d - 1
        zz[s, m, d].wait_recv()
        zf[s, m] = send(l_part(s, m, back), l_part(s, m, back), s_zf.at[s, m], r_zf.at[s, m], device(dz=-back))

    core, pair, to_core, to_y, fwd, outs = {}, {}, {}, {}, {}, []
    mine = pl.ds(pl.multiple_of(c * TOK, TOK), TOK)
    theirs = pl.ds(pl.multiple_of((1 - c) * TOK, TOK), TOK)

    def wait_r(p):
        local[2 + p].wait()
        for d in range(2):
            if d == 1:
                xa[p, d].wait_recv()
            else:
                xb[p, d].wait_recv()
            xf[p, d].wait_recv()

    def wait_l(s):
        local[s].wait()
        for m in range(4):
            zz[s, m, 1 - m // 2].wait_recv()
            zf[s, m].wait_recv()

    def compute(p):
        s = 0 if p < 3 else 1
        for l in range(2):
            right = rbuf[p].reshape(8 * TOK, HALF)

            def rows(rs):
                left = lbuf[s, l, :, :, :, rs].reshape(8 * TOK, TOK)
                part[p, l, rs, :] = lax.dot_general(
                    left, right, (((0,), (0,)), ((), ())), preferred_element_type=jnp.float32
                )

            rows(theirs)
            core[p, l] = send(
                part.at[p, l, theirs, :], core_in.at[p, l], s_core.at[p, l], r_core.at[p, l], device(other=True)
            )
            rows(mine)

    def reduce_cores(p):
        for l in range(2):
            core[p, l].wait_recv()
            part[p, l, mine, :] += core_in[p, l]
        pair[p] = send(part.at[p, 1 - yl, mine, :], pair_in.at[p], s_pair.at[p], r_pair.at[p], device(m=1))

    def lanes(value):
        return jnp.broadcast_to(value, (1, 128))

    def weight_sums():
        own_weights.start()
        own_weights.wait()
        for p in range(4):
            total = jnp.zeros((8, 1024), jnp.float32)
            for i in range(16):
                block = share[p, 8 * i : 8 * i + 8, :]
                total = total + block * block
            sum1[row_slot, 2, p : p + 1, :] = lanes(jnp.sum(total))

    def exact_dot(a, b, dims):
        return lax.dot_general(
            a, b, (dims, ((), ())), precision=lax.Precision.HIGHEST, preferred_element_type=jnp.float32
        )

    row_slot, col_slot = z * 2 + yh, x * 4 + yl * 2 + c

    def statistics(p):
        squares = final[p] * final[p] + 1e-30
        colx[col_slot, p : p + 1, :] = jnp.sum(squares, axis=0, keepdims=True)
        sums = exact_dot(jnp.ones((8, HALF), jnp.float32), squares, ((1,), (1,)))
        rowx[row_slot, p : p + 1, :] = sums[0:1]

    def exchange(buf, slot, peers, ss, rs):
        return [send(buf.at[slot], buf.at[slot], ss.at[k], rs.at[k], to) for k, to in peers]

    def landed(copies):
        for copy in copies:
            copy.wait_recv()

    def finish(p):
        pair[p].wait_recv()
        final[p] = part[p, yl, mine, :] + pair_in[p]
        statistics(p)
        if p == 3:
            stats.append(exchange(rowx, row_slot, row_peers, s_rx, r_rx))
            stats.append(exchange(colx, col_slot, col_peers, s_cx, r_cx))
        here = out.at[p, mine, columns(yh)]
        to_y[p] = send(final.at[p], here, s_gy.at[p], r_gy.at[p], device(m=2))
        to_core[p] = send(final.at[p], here, s_gc.at[p], r_gc.at[p], device(other=True))
        copy = pltpu.make_async_copy(final.at[p], here, s_out.at[p])
        copy.start()
        outs.append(copy)

    def forward(p):
        to_y[p].wait_recv()
        there = out.at[p, mine, columns(1 - yh)]
        fwd[p] = send(there, there, s_gf.at[p], r_gf.at[p], device(other=True))

    stats = []
    send_ry(0)
    for m in (1, 3, 2):
        send_ly(0, m)
    send_xa(0)
    send_z(0, 0)
    send_ry(1)
    send_z(1, 0)
    for m in (1, 3, 2):
        send_ly(1, m)
    send_ry(2)
    send_ry(3)
    weight_sums()
    send_xb(0)
    send_xa(1)
    for m in (1, 3, 2):
        send_z(0, m)
    send_xf(0)
    send_xb(1)
    send_xa(2)
    for m in (0, 1, 3, 2):
        send_zf(0, m)
    send_xf(1)
    send_xb(2)
    send_xa(3)
    for m in (1, 3, 2):
        send_z(1, m)
    wait_l(0)
    wait_r(0)
    compute(0)
    wait_r(1)
    compute(1)
    reduce_cores(0)
    reduce_cores(1)
    send_xf(2)
    send_xb(3)
    for m in (0, 1, 3, 2):
        send_zf(1, m)
    finish(0)
    wait_r(2)
    compute(2)
    send_xf(3)
    reduce_cores(2)
    finish(1)
    wait_l(1)
    wait_r(3)
    compute(3)
    reduce_cores(3)
    forward(0)
    finish(2)
    forward(1)
    finish(3)

    decay = 1.0 - float(STEP) ** (-0.8)
    landed(stats[0])
    sums = rowx[0]
    for k in range(1, 8):
        sums = sums + rowx[k]
    rows_new = decay * row_moment[:, mine] + (1.0 - decay) * (sums / D)
    rown[c] = rows_new
    to_rn = send(rown.at[c], rown.at[c], s_rn.at[0], r_rn.at[0], device(other=True))
    landed(stats[1])
    sums = colx[0]
    for k in range(1, 16):
        sums = sums + colx[k]
    cols_new = decay * col_moment[:, columns(yh)] + (1.0 - decay) * (sums / D)
    coln[yh] = cols_new
    to_cn = send(coln.at[yh], coln.at[yh], s_cn.at[0], r_cn.at[0], device(m=2))
    for p in range(4):
        sum1[row_slot, 0, p : p + 1, :] = lanes(jnp.sum(rows_new[p : p + 1]) * 0.125)
        by_row = jnp.broadcast_to(1.0 / rows_new[p : p + 1], (8, TOK))
        by_col = exact_dot(by_row, final[p] * final[p], ((1,), (0,)))
        sum1[row_slot, 1, p : p + 1, :] = lanes(jnp.sum(by_col[0:1] / cols_new[p : p + 1]))
    landed(exchange(sum1, row_slot, row_peers, s_s1, r_s1))
    sums = sum1[0]
    for k in range(1, 8):
        sums = sums + sum1[k]
    sum2[col_slot] = sums
    landed(exchange(sum2, col_slot, col_peers, s_s2, r_s2))
    sums = sum2[0]
    for k in range(1, 16):
        sums = sums + sum2[k]
    mean_row = sums[0] / D
    clip = jnp.maximum(1.0, jnp.sqrt(sums[1] * mean_row / (D * D)))
    size = min(0.01, float(STEP) ** (-0.5)) * jnp.maximum(0.001, jnp.sqrt(sums[2] / (D * D)))
    factor = (-(size / clip) * jnp.sqrt(mean_row))[:, 0:1]
    to_rn.wait_recv()
    to_cn.wait_recv()
    for k in range(2):
        out_row[:, TOK * k : TOK * (k + 1)] = rown[k]
        out_left[:, TOK * k : TOK * (k + 1)] = factor * lax.rsqrt(rown[k])
        out_col[:, HALF * k : HALF * (k + 1)] = coln[k]
        out_right[:, HALF * k : HALF * (k + 1)] = lax.rsqrt(coln[k])

    forward(2)
    forward(3)
    for p in range(4):
        to_core[p].wait_recv()
        fwd[p].wait_recv()
        outs[p].wait()
    for copy in sent:
        copy.wait_send()


def gradients(inputs, out_grads, weights, row_moment, col_moment):
    dma = pltpu.SemaphoreType.DMA
    any_space = pl.BlockSpec(memory_space=pl.ANY)
    vmem = pl.BlockSpec(memory_space=pltpu.VMEM)
    f32 = jnp.float32
    return pl.pallas_call(
        gradient_kernel,
        out_shape=[
            jax.ShapeDtypeStruct((4, 512, 1024), f32),
            jax.ShapeDtypeStruct((4, 512), f32),
            jax.ShapeDtypeStruct((4, 1024), f32),
            jax.ShapeDtypeStruct((4, 512), f32),
            jax.ShapeDtypeStruct((4, 1024), f32),
        ],
        in_specs=[any_space, any_space, any_space, vmem, vmem],
        out_specs=[any_space, vmem, vmem, vmem, vmem],
        scratch_shapes=[
            pltpu.VMEM((2, 2, 4, 2, TOK, HALF), jnp.bfloat16),
            pltpu.VMEM((4, 4, 2, TOK, HALF), jnp.bfloat16),
            pltpu.VMEM((4, 2, 512, HALF), f32),
            pltpu.VMEM((4, 2, TOK, HALF), f32),
            pltpu.VMEM((4, TOK, HALF), f32),
            pltpu.VMEM((4, TOK, HALF), f32),
            pltpu.VMEM((4, 128, 1024), f32),
            pltpu.VMEM((8, 4, TOK), f32),
            pltpu.VMEM((16, 4, HALF), f32),
            pltpu.VMEM((2, 4, TOK), f32),
            pltpu.VMEM((2, 4, HALF), f32),
            pltpu.VMEM((8, 3, 4, 128), f32),
            pltpu.VMEM((16, 3, 4, 128), f32),
            dma((6,)),
            dma((2, 3)), dma((2, 3)), dma((4,)), dma((4,)),
            dma((4, 2)), dma((4, 2)), dma((4, 2)), dma((4, 2)), dma((4, 2)), dma((4, 2)),
            dma((2, 4, 2)), dma((2, 4, 2)), dma((2, 4)), dma((2, 4)),
            dma((4, 2)), dma((4, 2)), dma((4,)), dma((4,)),
            dma((4,)), dma((4,)), dma((4,)), dma((4,)), dma((4,)), dma((4,)), dma((4,)),
            dma((1,)), dma((8,)), dma((8,)), dma((16,)), dma((16,)),
            dma((1,)), dma((1,)), dma((1,)), dma((1,)), dma((8,)), dma((8,)), dma((16,)), dma((16,)),
        ],
        name="gradients",
        compiler_params=pltpu.CompilerParams(
            collective_id=0, has_side_effects=True, vmem_limit_bytes=56 * 2**20
        ),
    )(inputs, out_grads, weights, row_moment, col_moment)


def local(inputs, out_grads, weights, row_moment, col_moment):
    gradient, row_new, col_new, left, right = gradients(inputs, out_grads, weights, row_moment, col_moment)
    return (gradient * (left[:, :, None] * right[:, None, :]), row_new, col_new)


def solution(mesh):
    return jax.shard_map(
        local,
        mesh=mesh,
        in_specs=(
            P(None, ("dp", "col"), "row"),
            P(None, ("dp", "row"), "col"),
            P(None, "row", "col"),
            P(None, "row"),
            P(None, "col"),
        ),
        out_specs=(P(None, "row", "col"), P(None, "row"), P(None, "col")),
        check_vma=False,
    )
```

```python
import jax
import jax.numpy as jnp
from jax import lax
from jax.experimental import pallas as pl
from jax.experimental.pallas import tpu as pltpu
from jax.sharding import PartitionSpec as P

D = 4096
STEP = 10
MESH = pl.DeviceIdType.MESH
TOK = 256
HALF = 512


TOP = 2.0**7.75


def encode(v):
    square = v * v
    fourth = square * square
    eighth = fourth * fourth
    power = eighth * eighth
    return jnp.where(v < 0, -power, power)


def decode(y):
    root = lax.rsqrt(lax.rsqrt(lax.rsqrt(lax.rsqrt(jnp.abs(y)))))
    return jnp.where(y == 0, 0.0, jnp.where(y < 0, -root, root))


def scale_kernel(code, left, right, out):
    col = jnp.transpose(left[0, 0])[:, 0:1]
    out[0] = decode(code[0].astype(jnp.float32)) * col * right[0]


def gradient_kernel(
    inputs, out_grads, weights, row_moment, col_moment, out, out_row, out_col, out_left, out_right,
    lbuf, rbuf, part, core_in, pair_in, final, code, share, rowx, colx, rown, coln, sum1, sum2,
    s_loc, s_ly, r_ly, s_ry, r_ry, s_xa, r_xa, s_xb, r_xb, s_xf, r_xf,
    s_z, r_z, s_zf, r_zf, s_core, r_core, s_pair, r_pair, s_gc, r_gc, s_gy, r_gy, s_gf, r_gf, s_out,
    s_share, s_rx, r_rx, s_cx, r_cx, s_rn, r_rn, s_cn, r_cn, s_s1, r_s1, s_s2, r_s2,
):
    dp, row, z = lax.axis_index("dp"), lax.axis_index("row"), lax.axis_index("col")
    yh, c, x, yl = dp // 2, dp % 2, row // 2, row % 2

    def device(dx=0, m=0, dz=0, other=False):
        h = 1 - yh if m & 2 else yh
        l = 1 - yl if m & 1 else yl
        return {
            "dp": h * 2 + (1 - c if other else c),
            "row": ((x + dx) % 4) * 2 + l,
            "col": (z + dz) % 4,
        }

    def send(src, dst, ss, rs, to):
        copy = pltpu.make_async_remote_copy(
            src_ref=src, dst_ref=dst, send_sem=ss, recv_sem=rs, device_id=to, device_id_type=MESH
        )
        copy.start()
        sent.append(copy)
        return copy

    sent = []
    row_peers = [(dz * 2 + h, device(dz=dz, m=2 * h)) for dz in range(4) for h in range(2) if dz + h]
    col_peers = [
        (dx * 4 + l * 2 + o, device(dx=dx, m=l, other=bool(o)))
        for dx in range(4) for l in range(2) for o in range(2) if dx + l + o
    ]
    neighbours = [to for _, to in row_peers + col_peers] + [device(m=3)]
    barrier = pltpu.get_barrier_semaphore()
    for other in neighbours:
        pl.semaphore_signal(barrier, inc=1, device_id=other, device_id_type=MESH)
    pl.semaphore_wait(barrier, len(neighbours))

    def flip(bit, value):
        return 1 - value if bit else value

    def token_rows(m):
        h = yl
        if (m >> 1) ^ (m & 1):
            h = 1 - yl
        return pl.ds(pl.multiple_of(h * TOK, TOK), TOK)

    def columns(h):
        return pl.ds(pl.multiple_of(h * HALF, HALF), HALF)

    def l_part(s, m, dz=0):
        return lbuf.at[s, flip(m & 1, yl), (z + dz) % 4, flip(m & 2, yh)]

    def r_part(p, m, dx=0):
        return rbuf.at[p, (x + dx) % 4, flip(m, yh)]

    quarter = pl.ds(pl.multiple_of(dp * 128, 128), 128)
    own_weights = pltpu.make_async_copy(weights.at[:, quarter, :], share, s_share.at[0])
    local = []
    for s in range(2):
        copy = pltpu.make_async_copy(inputs.at[s, token_rows(0), :], l_part(s, 0), s_loc.at[s])
        copy.start()
        local.append(copy)
    for p in range(4):
        copy = pltpu.make_async_copy(out_grads.at[p, :, columns(yh)], r_part(p, 0), s_loc.at[2 + p])
        copy.start()
        local.append(copy)

    ly, ry, xa, xb, xf, zz, zf = {}, {}, {}, {}, {}, {}, {}

    def send_ly(s, m):
        ly[s, m] = send(inputs.at[s, token_rows(m), :], l_part(s, 0), s_ly.at[s, m - 1], r_ly.at[s, m - 1], device(m=m))

    def send_ry(p):
        ry[p] = send(out_grads.at[p, :, columns(1 - yh)], r_part(p, 0), s_ry.at[p], r_ry.at[p], device(m=3))

    def send_xa(p):
        for d in range(2):
            xa[p, d] = send(out_grads.at[p, :, columns(yh)], r_part(p, 0), s_xa.at[p, d], r_xa.at[p, d], device(dx=1 - 2 * d))

    def send_xb(p):
        ry[p].wait_recv()
        for d in range(2):
            xb[p, d] = send(r_part(p, 1), r_part(p, 1), s_xb.at[p, d], r_xb.at[p, d], device(dx=1 - 2 * d))

    def send_xf(p):
        xa[p, 0].wait_recv()
        xf[p, 0] = send(r_part(p, 0, -1), r_part(p, 0, -1), s_xf.at[p, 0], r_xf.at[p, 0], device(dx=1))
        xb[p, 1].wait_recv()
        xf[p, 1] = send(r_part(p, 1, 1), r_part(p, 1, 1), s_xf.at[p, 1], r_xf.at[p, 1], device(dx=-1))

    def send_z(s, m):
        if m:
            ly[s, m].wait_recv()
        for d in range(2):
            src = l_part(s, m) if m else inputs.at[s, token_rows(0), :]
            zz[s, m, d] = send(src, l_part(s, m), s_z.at[s, m, d], r_z.at[s, m, d], device(dz=1 - 2 * d))

    def send_zf(s, m):
        d = m // 2
        back = 2 * d - 1
        zz[s, m, d].wait_recv()
        zf[s, m] = send(l_part(s, m, back), l_part(s, m, back), s_zf.at[s, m], r_zf.at[s, m], device(dz=-back))

    core, pair, to_core, to_y, fwd, outs = {}, {}, {}, {}, {}, []
    mine = pl.ds(pl.multiple_of(c * TOK, TOK), TOK)
    theirs = pl.ds(pl.multiple_of((1 - c) * TOK, TOK), TOK)

    def wait_r(p):
        local[2 + p].wait()
        for d in range(2):
            if d == 1:
                xa[p, d].wait_recv()
            else:
                xb[p, d].wait_recv()
            xf[p, d].wait_recv()

    def wait_l(s):
        local[s].wait()
        for m in range(4):
            zz[s, m, 1 - m // 2].wait_recv()
            zf[s, m].wait_recv()

    def compute(p):
        s = 0 if p < 3 else 1
        for l in range(2):
            right = rbuf[p].reshape(8 * TOK, HALF)

            def rows(rs):
                left = lbuf[s, l, :, :, :, rs].reshape(8 * TOK, TOK)
                part[p, l, rs, :] = lax.dot_general(
                    left, right, (((0,), (0,)), ((), ())), preferred_element_type=jnp.float32
                )

            rows(theirs)
            core[p, l] = send(
                part.at[p, l, theirs, :], core_in.at[p, l], s_core.at[p, l], r_core.at[p, l], device(other=True)
            )
            rows(mine)

    def reduce_cores(p):
        for l in range(2):
            core[p, l].wait_recv()
            part[p, l, mine, :] += core_in[p, l]
        pair[p] = send(part.at[p, 1 - yl, mine, :], pair_in.at[p], s_pair.at[p], r_pair.at[p], device(m=1))

    def lanes(value):
        return jnp.broadcast_to(value, (1, 128))

    def weight_sums():
        own_weights.start()
        own_weights.wait()
        for p in range(4):
            total = jnp.zeros((8, 1024), jnp.float32)
            for i in range(16):
                block = share[p, 8 * i : 8 * i + 8, :]
                total = total + block * block
            sum1[row_slot, 2, p : p + 1, :] = lanes(jnp.sum(total))

    def exact_dot(a, b, dims):
        return lax.dot_general(
            a, b, (dims, ((), ())), precision=lax.Precision.HIGHEST, preferred_element_type=jnp.float32
        )

    row_slot, col_slot = z * 2 + yh, x * 4 + yl * 2 + c

    def statistics(p):
        squares = final[p] * final[p] + 1e-30
        colx[col_slot, p : p + 1, :] = jnp.sum(squares, axis=0, keepdims=True)
        sums = exact_dot(jnp.ones((8, HALF), jnp.float32), squares, ((1,), (1,)))
        rowx[row_slot, p : p + 1, :] = sums[0:1]

    def exchange(buf, slot, peers, ss, rs):
        return [send(buf.at[slot], buf.at[slot], ss.at[k], rs.at[k], to) for k, to in peers]

    def landed(copies):
        for copy in copies:
            copy.wait_recv()

    def finish(p):
        pair[p].wait_recv()
        gradient = part[p, yl, mine, :] + pair_in[p]
        final[p] = gradient
        statistics(p)
        if p == 3:
            stats.append(exchange(rowx, row_slot, row_peers, s_rx, r_rx))
            stats.append(exchange(colx, col_slot, col_peers, s_cx, r_cx))
        norm = jnp.sum(gradient * gradient + 1e-30, axis=1, keepdims=True)
        code[p] = encode(gradient * (TOP * lax.rsqrt(norm))).astype(jnp.bfloat16)
        here = out.at[p, mine, columns(yh)]
        to_y[p] = send(code.at[p], here, s_gy.at[p], r_gy.at[p], device(m=2))
        to_core[p] = send(code.at[p], here, s_gc.at[p], r_gc.at[p], device(other=True))
        copy = pltpu.make_async_copy(code.at[p], here, s_out.at[p])
        copy.start()
        outs.append(copy)

    def forward(p):
        to_y[p].wait_recv()
        there = out.at[p, mine, columns(1 - yh)]
        fwd[p] = send(there, there, s_gf.at[p], r_gf.at[p], device(other=True))

    stats = []
    send_ry(0)
    for m in (1, 3, 2):
        send_ly(0, m)
    send_xa(0)
    send_z(0, 0)
    send_ry(1)
    send_z(1, 0)
    for m in (1, 3, 2):
        send_ly(1, m)
    send_ry(2)
    send_ry(3)
    weight_sums()
    send_xb(0)
    send_xa(1)
    for m in (1, 3, 2):
        send_z(0, m)
    send_xf(0)
    send_xb(1)
    send_xa(2)
    for m in (0, 1, 3, 2):
        send_zf(0, m)
    send_xf(1)
    send_xb(2)
    send_xa(3)
    for m in (1, 3, 2):
        send_z(1, m)
    wait_l(0)
    wait_r(0)
    compute(0)
    wait_r(1)
    compute(1)
    reduce_cores(0)
    reduce_cores(1)
    send_xf(2)
    send_xb(3)
    for m in (0, 1, 3, 2):
        send_zf(1, m)
    finish(0)
    wait_r(2)
    compute(2)
    send_xf(3)
    reduce_cores(2)
    finish(1)
    wait_l(1)
    wait_r(3)
    compute(3)
    reduce_cores(3)
    forward(0)
    finish(2)
    forward(1)
    finish(3)

    decay = 1.0 - float(STEP) ** (-0.8)
    landed(stats[0])
    sums = rowx[0]
    for k in range(1, 8):
        sums = sums + rowx[k]
    rows_new = decay * row_moment[:, mine] + (1.0 - decay) * (sums / D)
    rown[c, 0] = rows_new
    for h in range(2):
        rown[c, 1 + h] = rowx[z * 2 + h]
    to_rn = send(rown.at[c], rown.at[c], s_rn.at[0], r_rn.at[0], device(other=True))
    landed(stats[1])
    sums = colx[0]
    for k in range(1, 16):
        sums = sums + colx[k]
    cols_new = decay * col_moment[:, columns(yh)] + (1.0 - decay) * (sums / D)
    coln[yh] = cols_new
    to_cn = send(coln.at[yh], coln.at[yh], s_cn.at[0], r_cn.at[0], device(m=2))
    for p in range(4):
        sum1[row_slot, 0, p : p + 1, :] = lanes(jnp.sum(rows_new[p : p + 1]) * 0.125)
        by_row = jnp.broadcast_to(1.0 / rows_new[p : p + 1], (8, TOK))
        by_col = exact_dot(by_row, final[p] * final[p], ((1,), (0,)))
        sum1[row_slot, 1, p : p + 1, :] = lanes(jnp.sum(by_col[0:1] / cols_new[p : p + 1]))
    landed(exchange(sum1, row_slot, row_peers, s_s1, r_s1))
    sums = sum1[0]
    for k in range(1, 8):
        sums = sums + sum1[k]
    sum2[col_slot] = sums
    landed(exchange(sum2, col_slot, col_peers, s_s2, r_s2))
    sums = sum2[0]
    for k in range(1, 16):
        sums = sums + sum2[k]
    mean_row = sums[0] / D
    clip = jnp.maximum(1.0, jnp.sqrt(sums[1] * mean_row / (D * D)))
    size = min(0.01, float(STEP) ** (-0.5)) * jnp.maximum(0.001, jnp.sqrt(sums[2] / (D * D)))
    factor = (-(size / clip) * jnp.sqrt(mean_row))[:, 0:1]
    to_rn.wait_recv()
    to_cn.wait_recv()
    for k in range(2):
        out_row[:, TOK * k : TOK * (k + 1)] = rown[k, 0]
        for h in range(2):
            rows_left = factor * lax.rsqrt(rown[k, 0]) * jnp.sqrt(rown[k, 1 + h]) * (1.0 / TOP)
            for p in range(4):
                out_left[p, h, :, TOK * k : TOK * (k + 1)] = jnp.broadcast_to(rows_left[p : p + 1], (8, TOK))
        out_col[:, HALF * k : HALF * (k + 1)] = coln[k]
        cols_right = lax.rsqrt(coln[k])
        for p in range(4):
            out_right[p, :, HALF * k : HALF * (k + 1)] = cols_right[p : p + 1]

    forward(2)
    forward(3)
    for p in range(4):
        to_core[p].wait_recv()
        fwd[p].wait_recv()
        outs[p].wait()
    for copy in sent:
        copy.wait_send()


def gradients(inputs, out_grads, weights, row_moment, col_moment):
    dma = pltpu.SemaphoreType.DMA
    any_space = pl.BlockSpec(memory_space=pl.ANY)
    vmem = pl.BlockSpec(memory_space=pltpu.VMEM)
    f32 = jnp.float32
    return pl.pallas_call(
        gradient_kernel,
        out_shape=[
            jax.ShapeDtypeStruct((4, 512, 1024), jnp.bfloat16),
            jax.ShapeDtypeStruct((4, 512), f32),
            jax.ShapeDtypeStruct((4, 1024), f32),
            jax.ShapeDtypeStruct((4, 2, 8, 512), f32),
            jax.ShapeDtypeStruct((4, 1, 1024), f32),
        ],
        in_specs=[any_space, any_space, any_space, vmem, vmem],
        out_specs=[any_space, vmem, vmem, vmem, vmem],
        scratch_shapes=[
            pltpu.VMEM((2, 2, 4, 2, TOK, HALF), jnp.bfloat16),
            pltpu.VMEM((4, 4, 2, TOK, HALF), jnp.bfloat16),
            pltpu.VMEM((4, 2, 512, HALF), f32),
            pltpu.VMEM((4, 2, TOK, HALF), f32),
            pltpu.VMEM((4, TOK, HALF), f32),
            pltpu.VMEM((4, TOK, HALF), f32),
            pltpu.VMEM((4, TOK, HALF), jnp.bfloat16),
            pltpu.VMEM((4, 128, 1024), f32),
            pltpu.VMEM((8, 4, TOK), f32),
            pltpu.VMEM((16, 4, HALF), f32),
            pltpu.VMEM((2, 3, 4, TOK), f32),
            pltpu.VMEM((2, 4, HALF), f32),
            pltpu.VMEM((8, 3, 4, 128), f32),
            pltpu.VMEM((16, 3, 4, 128), f32),
            dma((6,)),
            dma((2, 3)), dma((2, 3)), dma((4,)), dma((4,)),
            dma((4, 2)), dma((4, 2)), dma((4, 2)), dma((4, 2)), dma((4, 2)), dma((4, 2)),
            dma((2, 4, 2)), dma((2, 4, 2)), dma((2, 4)), dma((2, 4)),
            dma((4, 2)), dma((4, 2)), dma((4,)), dma((4,)),
            dma((4,)), dma((4,)), dma((4,)), dma((4,)), dma((4,)), dma((4,)), dma((4,)),
            dma((1,)), dma((8,)), dma((8,)), dma((16,)), dma((16,)),
            dma((1,)), dma((1,)), dma((1,)), dma((1,)), dma((8,)), dma((8,)), dma((16,)), dma((16,)),
        ],
        name="gradients",
        compiler_params=pltpu.CompilerParams(
            collective_id=0, has_side_effects=True, vmem_limit_bytes=56 * 2**20
        ),
    )(inputs, out_grads, weights, row_moment, col_moment)


def local(inputs, out_grads, weights, row_moment, col_moment):
    code, row_new, col_new, left, right = gradients(inputs, out_grads, weights, row_moment, col_moment)
    change = pl.pallas_call(
        scale_kernel,
        out_shape=jax.ShapeDtypeStruct((4, 512, 1024), jnp.float32),
        grid=(4, 2),
        in_specs=[
            pl.BlockSpec((1, 512, HALF), lambda p, h: (p, 0, h)),
            pl.BlockSpec((1, 1, 8, 512), lambda p, h: (p, h, 0, 0)),
            pl.BlockSpec((1, 1, HALF), lambda p, h: (p, 0, h)),
        ],
        out_specs=pl.BlockSpec((1, 512, HALF), lambda p, h: (p, 0, h)),
        name="scale",
    )(code, left, right)
    return (change, row_new, col_new)


def solution(mesh):
    return jax.shard_map(
        local,
        mesh=mesh,
        in_specs=(
            P(None, ("dp", "col"), "row"),
            P(None, ("dp", "row"), "col"),
            P(None, "row", "col"),
            P(None, "row"),
            P(None, "col"),
        ),
        out_specs=(P(None, "row", "col"), P(None, "row"), P(None, "col")),
        check_vma=False,
    )
```

```python
import jax
import jax.numpy as jnp
from jax import lax
from jax.experimental import pallas as pl
from jax.experimental.pallas import tpu as pltpu
from jax.sharding import PartitionSpec as P

D = 4096
STEP = 10
MESH = pl.DeviceIdType.MESH
TOK = 256
HALF = 512


TOP = 2.0**7.75


def encode(v):
    square = v * v
    fourth = square * square
    eighth = fourth * fourth
    power = eighth * eighth
    return jnp.where(v < 0, -power, power)


def decode(y):
    return y * jnp.exp2(jnp.log2(jnp.maximum(jnp.abs(y), 1e-37)) * (-15.0 / 16.0))


def scale_kernel(
    code, left_in, right_in, row_new, col_new, out, out_row, out_col, codes, changes, left, right, s_in, s_out, s_small
):
    blocks = [(p, i) for p in range(4) for i in range(2)]
    rows = [pl.ds(TOK * i, TOK) for i in range(2)]
    loads = [pltpu.make_async_copy(code.at[p, rows[i]], codes.at[p, rows[i]], s_in.at[p, i]) for p, i in blocks]
    stores = [pltpu.make_async_copy(changes.at[p, rows[i]], out.at[p, rows[i]], s_out.at[p, i]) for p, i in blocks]
    small = [
        pltpu.make_async_copy(a, b, s_small.at[k])
        for k, (a, b) in enumerate([(left_in, left), (right_in, right), (row_new, out_row), (col_new, out_col)])
    ]
    for load in small + loads:
        load.start()
    small[0].wait()
    small[1].wait()
    for k, (p, i) in enumerate(blocks):
        loads[k].wait()
        for h in range(2):
            cols = pl.ds(HALF * h, HALF)
            col = jnp.transpose(left[p, h, :, rows[i]])[:, 0:1]
            changes[p, rows[i], cols] = decode(codes[p, rows[i], cols].astype(jnp.float32)) * (col * right[p, :, cols])
        stores[k].start()
    for store in stores + small[2:]:
        store.wait()


def gradient_kernel(
    inputs, out_grads, weights, row_moment, col_moment, out, out_row, out_col, out_left, out_right,
    lbuf, rbuf, part, core_in, pair_in, final, code, share, rowx, colx, dcolx, rown, coln, sum1, sum2,
    s_loc, s_ly, r_ly, s_ry, r_ry, s_xa, r_xa, s_xb, r_xb, s_xf, r_xf,
    s_z, r_z, s_zf, r_zf, s_core, r_core, s_pair, r_pair, s_gc, r_gc, s_gy, r_gy, s_gf, r_gf, s_out,
    s_share, s_rx, r_rx, s_cx, r_cx, s_dx, r_dx, s_rn, r_rn, s_cn, r_cn, s_s1, r_s1, s_s2, r_s2,
):
    dp, row, z = lax.axis_index("dp"), lax.axis_index("row"), lax.axis_index("col")
    yh, c, x, yl = dp // 2, dp % 2, row // 2, row % 2

    def device(dx=0, m=0, dz=0, other=False):
        h = 1 - yh if m & 2 else yh
        l = 1 - yl if m & 1 else yl
        return {
            "dp": h * 2 + (1 - c if other else c),
            "row": ((x + dx) % 4) * 2 + l,
            "col": (z + dz) % 4,
        }

    def send(src, dst, ss, rs, to):
        copy = pltpu.make_async_remote_copy(
            src_ref=src, dst_ref=dst, send_sem=ss, recv_sem=rs, device_id=to, device_id_type=MESH
        )
        copy.start()
        sent.append(copy)
        return copy

    sent, drained = [], [0]

    def drain(count):
        for copy in sent[drained[0] : count]:
            copy.wait_send()
        drained[0] = max(drained[0], count)

    half = [yh, (yh + yl) % 2, yh, (yh + yl) % 2]
    row_peers = [(dz * 2 + h, device(dz=dz, m=2 * h)) for dz in range(4) for h in range(2) if dz + h]
    col_peers = [
        (dx * 4 + l * 2 + o, device(dx=dx, m=l, other=bool(o)))
        for dx in range(4) for l in range(2) for o in range(2) if dx + l + o
    ]
    diagonal_peers = [
        (dx * 4 + l * 2 + o, device(dx=dx, m=3 * l, other=bool(o)))
        for dx in range(4) for l in range(2) for o in range(2) if dx + l + o
    ]
    plane_peers = [(dx * 4 + dz, device(dx=dx, dz=dz)) for dx in range(4) for dz in range(4) if dx + dz]
    line_peers = [(m * 2 + o, device(m=m, other=bool(o))) for m in range(4) for o in range(2) if m + o]
    neighbours = [to for _, to in row_peers + col_peers] + [to for k, to in diagonal_peers if k & 2]
    neighbours += [to for k, to in plane_peers if k // 4 and k % 4] + [to for k, to in line_peers if k == 5]
    barrier = pltpu.get_barrier_semaphore()
    for other in neighbours:
        pl.semaphore_signal(barrier, inc=1, device_id=other, device_id_type=MESH)
    pl.semaphore_wait(barrier, len(neighbours))

    def flip(bit, value):
        return 1 - value if bit else value

    def columns(h):
        return pl.ds(pl.multiple_of(h * HALF, HALF), HALF)

    def l_part(s, m, dz=0):
        return lbuf.at[s, flip(m & 1, yl), (z + dz) % 4, flip(m & 2, yh)]

    def r_part(p, m, dx=0):
        return rbuf.at[p, (x + dx) % 4, flip(m, yh)]

    def own_tokens(h):
        return pl.ds(pl.multiple_of(h * TOK, TOK), TOK)

    quarter = pl.ds(pl.multiple_of(dp * 128, 128), 128)
    own_weights = pltpu.make_async_copy(weights.at[:, quarter, :], share, s_share.at[0])
    local = []
    for s in range(2):
        copy = pltpu.make_async_copy(inputs.at[s, own_tokens(yl), :], l_part(s, 0), s_loc.at[s])
        copy.start()
        local.append(copy)
    for p in range(4):
        copy = pltpu.make_async_copy(out_grads.at[p, :, columns(half[p])], r_part(p, 0), s_loc.at[2 + p])
        copy.start()
        local.append(copy)

    ly, ry, xa, xb, xf, zz, zf = {}, {}, {}, {}, {}, {}, {}

    def send_ly(s, m):
        rows = own_tokens(flip(m & 1, yl))
        ly[s, m] = send(inputs.at[s, rows, :], l_part(s, 0), s_ly.at[s, m - 1], r_ly.at[s, m - 1], device(m=m))

    def send_ry(p):
        ry[p] = send(out_grads.at[p, :, columns(1 - half[p])], r_part(p, 0), s_ry.at[p], r_ry.at[p], device(m=2))

    def send_xa(p, ways=(0, 1)):
        for d in ways:
            xa[p, d] = send(out_grads.at[p, :, columns(half[p])], r_part(p, 0), s_xa.at[p, d], r_xa.at[p, d], device(dx=1 - 2 * d))

    def send_xb(p, ways=(0, 1)):
        if not [k for k in xb if k[0] == p]:
            ry[p].wait_recv()
        for d in ways:
            xb[p, d] = send(r_part(p, 1), r_part(p, 1), s_xb.at[p, d], r_xb.at[p, d], device(dx=1 - 2 * d))

    def send_xfa(p):
        xa[p, 0].wait_recv()
        xf[p, 0] = send(r_part(p, 0, -1), r_part(p, 0, -1), s_xf.at[p, 0], r_xf.at[p, 0], device(dx=1))

    def send_xfb(p):
        xb[p, 1].wait_recv()
        xf[p, 1] = send(r_part(p, 1, 1), r_part(p, 1, 1), s_xf.at[p, 1], r_xf.at[p, 1], device(dx=-1))

    def send_z(s, m):
        if m:
            ly[s, m].wait_recv()
        for d in range(2):
            src = l_part(s, m) if m else inputs.at[s, own_tokens(yl), :]
            zz[s, m, d] = send(src, l_part(s, m), s_z.at[s, m, d], r_z.at[s, m, d], device(dz=1 - 2 * d))

    def send_zf(s, m):
        d = m // 2
        back = 2 * d - 1
        zz[s, m, d].wait_recv()
        zf[s, m] = send(l_part(s, m, back), l_part(s, m, back), s_zf.at[s, m], r_zf.at[s, m], device(dz=-back))

    core, pair, to_core, to_y, fwd, outs = {}, {}, {}, {}, {}, []
    mine = pl.ds(pl.multiple_of(c * TOK, TOK), TOK)
    theirs = pl.ds(pl.multiple_of((1 - c) * TOK, TOK), TOK)

    def wait_r(p):
        local[2 + p].wait()
        for d in range(2):
            if d == 1:
                xa[p, d].wait_recv()
            else:
                xb[p, d].wait_recv()
            xf[p, d].wait_recv()

    def wait_l(s):
        local[s].wait()
        for m in range(4):
            zz[s, m, 1 - m // 2].wait_recv()
            zf[s, m].wait_recv()

    def compute(p):
        s = 0 if p < 3 else 1
        right = rbuf[p].reshape(8 * TOK, HALF)

        def rows(l, rs):
            left = lbuf[s, l, :, :, :, rs].reshape(8 * TOK, TOK)
            part[p, l, rs, :] = lax.dot_general(
                left, right, (((0,), (0,)), ((), ())), preferred_element_type=jnp.float32
            )

        to = device(m=3 if p % 2 else 1)
        for k, l in enumerate((1 - yl, yl)):
            rows(l, theirs)
            core[p, k] = send(
                part.at[p, l, theirs, :], core_in.at[p, l], s_core.at[p, k], r_core.at[p, k], device(other=True)
            )
            rows(l, mine)
            core[p, k].wait_recv()
            part[p, l, mine, :] += core_in[p, l]
            if k == 0:
                pair[p] = send(part.at[p, l, mine, :], pair_in.at[p], s_pair.at[p], r_pair.at[p], to)

    def lanes(value):
        return jnp.broadcast_to(value, (1, 128))

    def weight_sums():
        own_weights.wait()
        for p in range(4):
            total = jnp.zeros((8, 1024), jnp.float32)
            for i in range(16):
                block = share[p, 8 * i : 8 * i + 8, :]
                total = total + block * block
            sum1[plane_slot, 2, p : p + 1, :] = lanes(jnp.sum(total))

    def exact_dot(a, b, dims):
        return lax.dot_general(
            a, b, (dims, ((), ())), precision=lax.Precision.HIGHEST, preferred_element_type=jnp.float32
        )

    plane_slot, line_slot = x * 4 + z, dp * 2 + yl
    row_slot, col_slot, dcol_slot = z * 2 + yh, x * 4 + yl * 2 + c, x * 4 + yh * 2 + c

    def statistics(p):
        squares = final[p] * final[p] + 1e-30
        sums = jnp.sum(squares, axis=0, keepdims=True)
        if p % 2:
            dcolx[dcol_slot, p // 2 : p // 2 + 1, :] = sums
        else:
            colx[col_slot, p // 2 : p // 2 + 1, :] = sums
        sums = exact_dot(jnp.ones((8, HALF), jnp.float32), squares, ((1,), (1,)))
        rowx[row_slot, p : p + 1, :] = sums[0:1]

    def exchange(buf, slot, peers, ss, rs):
        return [send(buf.at[slot], buf.at[slot], ss.at[k], rs.at[k], to) for k, to in peers]

    def landed(copies):
        for copy in copies:
            copy.wait_recv()

    def hand_on(p):
        here = out.at[p, mine, columns(half[p])]
        to_y[p] = send(code.at[p], here, s_gy.at[p], r_gy.at[p], device(m=2))
        to_core[p] = send(code.at[p], here, s_gc.at[p], r_gc.at[p], device(other=True))
        copy = pltpu.make_async_copy(code.at[p], here, s_out.at[p])
        copy.start()
        outs.append(copy)

    def finish(p):
        pair[p].wait_recv()
        gradient = part[p, yl, mine, :] + pair_in[p]
        final[p] = gradient
        statistics(p)
        if p == 2:
            stats.append(exchange(colx, col_slot, col_peers, s_cx, r_cx))
        if p == 3:
            stats.append(exchange(rowx, row_slot, row_peers, s_rx, r_rx))
            stats.append(exchange(dcolx, dcol_slot, diagonal_peers, s_dx, r_dx))
        norm = jnp.sum(gradient * gradient + 1e-30, axis=1, keepdims=True)
        code[p] = encode(gradient * (TOP * lax.rsqrt(norm))).astype(jnp.bfloat16)

    def forward(p):
        to_y[p].wait_recv()
        there = out.at[p, mine, columns(1 - half[p])]
        fwd[p] = send(there, there, s_gf.at[p], r_gf.at[p], device(other=True))

    stats = []
    send_ly(0, 1)
    send_ly(0, 3)
    send_xa(0)
    send_z(0, 0)
    send_xa(1)
    own_weights.start()
    send_z(0, 1)
    send_z(0, 3)
    send_ry(0)
    send_ly(0, 2)
    send_ry(1)
    send_xa(2)
    weight_sums()
    send_xb(0)
    send_xfa(0)
    send_z(0, 2)
    send_zf(0, 0)
    send_zf(0, 1)
    send_xfb(0)
    send_ry(2)
    send_xb(1)
    send_zf(0, 3)
    send_zf(0, 2)
    send_xfa(1)
    send_ly(1, 1)
    send_ly(1, 3)
    send_ly(1, 2)
    send_ry(3)
    send_z(1, 0)
    send_xfb(1)
    send_xb(2)
    send_xa(3, (0,))
    send_z(1, 1)
    early = len(sent) - 12
    wait_r(0)
    wait_l(0)
    compute(0)
    send_z(1, 3)
    send_xb(3, (1,))
    send_xfa(2)
    wait_r(1)
    compute(1)
    send_z(1, 2)
    send_xfb(2)
    send_xa(3, (1,))
    send_xb(3, (0,))
    send_zf(1, 0)
    send_zf(1, 1)
    send_zf(1, 3)
    drain(early // 2)
    finish(0)
    hand_on(0)
    send_zf(1, 2)
    send_xfa(3)
    send_xfb(3)
    drain(early)
    finish(1)
    hand_on(1)
    wait_r(2)
    late = len(sent) - 6
    compute(2)
    wait_r(3)
    wait_l(1)
    compute(3)
    drain(late)
    forward(0)
    finish(2)
    finish(3)
    hand_on(2)
    hand_on(3)

    decay = 1.0 - float(STEP) ** (-0.8)
    tail = len(sent)
    landed(stats[1])
    sums = rowx[0]
    for k in range(1, 8):
        sums = sums + rowx[k]
    rows_new = decay * row_moment[:, mine] + (1.0 - decay) * (sums / D)
    rown[c, 0] = rows_new
    for h in range(2):
        rown[c, 1 + h] = rowx[z * 2 + h]
    to_rn = send(rown.at[c], rown.at[c], s_rn.at[0], r_rn.at[0], device(other=True))
    landed(stats[0])
    sums = colx[0]
    for k in range(1, 16):
        sums = sums + colx[k]
    for p in (0, 2):
        old = col_moment[p : p + 1, columns(half[p])]
        coln[yh, p : p + 1, :] = decay * old + (1.0 - decay) * (sums[p // 2 : p // 2 + 1] / D)
    landed(stats[2])
    sums = dcolx[0]
    for k in range(1, 16):
        sums = sums + dcolx[k]
    for p in (1, 3):
        old = col_moment[p : p + 1, columns(half[p])]
        coln[yh, p : p + 1, :] = decay * old + (1.0 - decay) * (sums[p // 2 : p // 2 + 1] / D)
    cols_new = coln[yh]
    to_cn = send(coln.at[yh], coln.at[yh], s_cn.at[0], r_cn.at[0], device(m=2))
    for p in range(4):
        sum1[plane_slot, 0, p : p + 1, :] = lanes(jnp.sum(rows_new[p : p + 1]) * 0.125)
        by_row = jnp.broadcast_to(1.0 / rows_new[p : p + 1], (8, TOK))
        by_col = exact_dot(by_row, final[p] * final[p], ((1,), (0,)))
        sum1[plane_slot, 1, p : p + 1, :] = lanes(jnp.sum(by_col[0:1] / cols_new[p : p + 1]))
    landed(exchange(sum1, plane_slot, plane_peers, s_s1, r_s1))
    sums = sum1[0]
    for k in range(1, 16):
        sums = sums + sum1[k]
    sum2[line_slot] = sums
    lines = exchange(sum2, line_slot, line_peers, s_s2, r_s2)
    drain(tail)
    forward(1)
    forward(2)
    forward(3)
    landed(lines)
    sums = sum2[0]
    for k in range(1, 8):
        sums = sums + sum2[k]
    mean_row = sums[0] / D
    clip = jnp.maximum(1.0, jnp.sqrt(sums[1] * mean_row / (D * D)))
    size = min(0.01, float(STEP) ** (-0.5)) * jnp.maximum(0.001, jnp.sqrt(sums[2] / (D * D)))
    factor = (-(size / clip) * jnp.sqrt(mean_row))[:, 0:1]
    to_rn.wait_recv()
    to_cn.wait_recv()
    for k in range(2):
        out_row[:, TOK * k : TOK * (k + 1)] = rown[k, 0]
        for h in range(2):
            rows_left = factor * lax.rsqrt(rown[k, 0]) * jnp.sqrt(rown[k, 1 + h]) * (1.0 / TOP)
            for p in range(4):
                out_left[p, (h + yl) % 2 if p % 2 else h, :, TOK * k : TOK * (k + 1)] = jnp.broadcast_to(rows_left[p : p + 1], (8, TOK))
        cols_right = lax.rsqrt(coln[k])
        for p in range(4):
            place = columns((k + yl) % 2) if p % 2 else pl.ds(HALF * k, HALF)
            out_col[p : p + 1, place] = coln[k, p : p + 1, :]
            out_right[p, :, place] = cols_right[p : p + 1]

    for p in range(4):
        to_core[p].wait_recv()
        fwd[p].wait_recv()
        outs[p].wait()
    drain(len(sent))


def gradients(inputs, out_grads, weights, row_moment, col_moment):
    dma = pltpu.SemaphoreType.DMA
    any_space = pl.BlockSpec(memory_space=pl.ANY)
    vmem = pl.BlockSpec(memory_space=pltpu.VMEM)
    f32 = jnp.float32
    return pl.pallas_call(
        gradient_kernel,
        out_shape=[
            jax.ShapeDtypeStruct((4, 512, 1024), jnp.bfloat16),
            jax.ShapeDtypeStruct((4, 512), f32),
            jax.ShapeDtypeStruct((4, 1024), f32),
            jax.ShapeDtypeStruct((4, 2, 8, 512), f32),
            jax.ShapeDtypeStruct((4, 1, 1024), f32),
        ],
        in_specs=[any_space, any_space, any_space, vmem, vmem],
        out_specs=[any_space, vmem, vmem, vmem, vmem],
        scratch_shapes=[
            pltpu.VMEM((2, 2, 4, 2, TOK, HALF), jnp.bfloat16),
            pltpu.VMEM((4, 4, 2, TOK, HALF), jnp.bfloat16),
            pltpu.VMEM((4, 2, 512, HALF), f32),
            pltpu.VMEM((4, 2, TOK, HALF), f32),
            pltpu.VMEM((4, TOK, HALF), f32),
            pltpu.VMEM((4, TOK, HALF), f32),
            pltpu.VMEM((4, TOK, HALF), jnp.bfloat16),
            pltpu.VMEM((4, 128, 1024), f32),
            pltpu.VMEM((8, 4, TOK), f32),
            pltpu.VMEM((16, 2, HALF), f32),
            pltpu.VMEM((16, 2, HALF), f32),
            pltpu.VMEM((2, 3, 4, TOK), f32),
            pltpu.VMEM((2, 4, HALF), f32),
            pltpu.VMEM((16, 3, 4, 128), f32),
            pltpu.VMEM((8, 3, 4, 128), f32),
            dma((6,)),
            dma((2, 3)), dma((2, 3)), dma((4,)), dma((4,)),
            dma((4, 2)), dma((4, 2)), dma((4, 2)), dma((4, 2)), dma((4, 2)), dma((4, 2)),
            dma((2, 4, 2)), dma((2, 4, 2)), dma((2, 4)), dma((2, 4)),
            dma((4, 2)), dma((4, 2)), dma((4,)), dma((4,)),
            dma((4,)), dma((4,)), dma((4,)), dma((4,)), dma((4,)), dma((4,)), dma((4,)),
            dma((1,)), dma((8,)), dma((8,)), dma((16,)), dma((16,)), dma((16,)), dma((16,)),
            dma((1,)), dma((1,)), dma((1,)), dma((1,)), dma((16,)), dma((16,)), dma((8,)), dma((8,)),
        ],
        name="gradients",
        compiler_params=pltpu.CompilerParams(
            collective_id=0, has_side_effects=True, vmem_limit_bytes=56 * 2**20
        ),
    )(inputs, out_grads, weights, row_moment, col_moment)


def local(inputs, out_grads, weights, row_moment, col_moment):
    code, row_new, col_new, left, right = gradients(inputs, out_grads, weights, row_moment, col_moment)
    any_space = pl.BlockSpec(memory_space=pl.ANY)
    f32 = jnp.float32
    return pl.pallas_call(
        scale_kernel,
        out_shape=[
            jax.ShapeDtypeStruct((4, 512, 1024), f32),
            jax.ShapeDtypeStruct((4, 512), f32),
            jax.ShapeDtypeStruct((4, 1024), f32),
        ],
        in_specs=[any_space] * 5,
        out_specs=[any_space] * 3,
        scratch_shapes=[
            pltpu.VMEM((4, 512, 1024), jnp.bfloat16),
            pltpu.VMEM((4, 512, 1024), f32),
            pltpu.VMEM((4, 2, 8, 512), f32),
            pltpu.VMEM((4, 1, 1024), f32),
            pltpu.SemaphoreType.DMA((4, 2)),
            pltpu.SemaphoreType.DMA((4, 2)),
            pltpu.SemaphoreType.DMA((4,)),
        ],
        name="scale",
        compiler_params=pltpu.CompilerParams(vmem_limit_bytes=60 * 2**20),
    )(code, left, right, row_new, col_new)


def solution(mesh):
    return jax.shard_map(
        local,
        mesh=mesh,
        in_specs=(
            P(None, ("dp", "col"), "row"),
            P(None, ("dp", "row"), "col"),
            P(None, "row", "col"),
            P(None, "row"),
            P(None, "col"),
        ),
        out_specs=(P(None, "row", "col"), P(None, "row"), P(None, "col")),
        check_vma=False,
    )
```

```python
import jax
import jax.numpy as jnp
from jax import lax
from jax.experimental import pallas as pl
from jax.experimental.pallas import tpu as pltpu
from jax.sharding import PartitionSpec as P

D = 4096
STEP = 10
MESH = pl.DeviceIdType.MESH
TOK = 256
HALF = 512


TOP = 2.0**7.75


def encode(v):
    square = v * v
    fourth = square * square
    eighth = fourth * fourth
    power = eighth * eighth
    return jnp.where(v < 0, -power, power)


def decode(y):
    return y * jnp.exp2(jnp.log2(jnp.maximum(jnp.abs(y), 1e-37)) * (-15.0 / 16.0))


def scale_kernel(
    code, left_in, right_in, row_new, col_new, out, out_row, out_col, codes, changes, left, right, s_in, s_out, s_small
):
    blocks = [(p, i) for p in range(4) for i in range(2)]
    rows = [pl.ds(TOK * i, TOK) for i in range(2)]
    loads = [pltpu.make_async_copy(code.at[p, rows[i]], codes.at[p, rows[i]], s_in.at[p, i]) for p, i in blocks]
    stores = [pltpu.make_async_copy(changes.at[p, rows[i]], out.at[p, rows[i]], s_out.at[p, i]) for p, i in blocks]
    small = [
        pltpu.make_async_copy(a, b, s_small.at[k])
        for k, (a, b) in enumerate([(left_in, left), (right_in, right), (row_new, out_row), (col_new, out_col)])
    ]
    for load in small + loads:
        load.start()
    small[0].wait()
    small[1].wait()
    for k, (p, i) in enumerate(blocks):
        loads[k].wait()
        for h in range(2):
            cols = pl.ds(HALF * h, HALF)
            col = jnp.transpose(left[p, h, :, rows[i]])[:, 0:1]
            changes[p, rows[i], cols] = decode(codes[p, rows[i], cols].astype(jnp.float32)) * (col * right[p, :, cols])
        stores[k].start()
    for store in stores + small[2:]:
        store.wait()


def gradient_kernel(
    inputs, out_grads, weights, row_moment, col_moment, out, out_row, out_col, out_left, out_right,
    lbuf, rbuf, part, core_in, pair_in, final, code, share, rowx, colx, dcolx, rown, coln, sum1, sum2,
    s_loc, s_ly, r_ly, s_ry, r_ry, s_xa, r_xa, s_xb, r_xb, s_xf, r_xf,
    s_z, r_z, s_zf, r_zf, s_core, r_core, s_pair, r_pair, s_gc, r_gc, s_gy, r_gy, s_gf, r_gf, s_out,
    s_share, s_rx, r_rx, s_cx, r_cx, s_dx, r_dx, s_rn, r_rn, s_cn, r_cn, s_s1, r_s1, s_s2, r_s2,
):
    dp, row, z = lax.axis_index("dp"), lax.axis_index("row"), lax.axis_index("col")
    yh, c, x, yl = dp // 2, dp % 2, row // 2, row % 2

    def device(dx=0, m=0, dz=0, other=False):
        h = 1 - yh if m & 2 else yh
        l = 1 - yl if m & 1 else yl
        return {
            "dp": h * 2 + (1 - c if other else c),
            "row": ((x + dx) % 4) * 2 + l,
            "col": (z + dz) % 4,
        }

    def send(src, dst, ss, rs, to):
        copy = pltpu.make_async_remote_copy(
            src_ref=src, dst_ref=dst, send_sem=ss, recv_sem=rs, device_id=to, device_id_type=MESH
        )
        copy.start()
        sent.append(copy)
        return copy

    sent, drained = [], [0]

    def drain(count):
        for copy in sent[drained[0] : count]:
            copy.wait_send()
        drained[0] = max(drained[0], count)

    half = [yh, (yh + yl) % 2, yh, (yh + yl) % 2]
    row_peers = [(dz * 2 + h, device(dz=dz, m=2 * h)) for dz in range(4) for h in range(2) if dz + h]
    col_peers = [
        (dx * 4 + l * 2 + o, device(dx=dx, m=l, other=bool(o)))
        for dx in range(4) for l in range(2) for o in range(2) if dx + l + o
    ]
    diagonal_peers = [
        (dx * 4 + l * 2 + o, device(dx=dx, m=3 * l, other=bool(o)))
        for dx in range(4) for l in range(2) for o in range(2) if dx + l + o
    ]
    plane_peers = [(dx * 4 + dz, device(dx=dx, dz=dz)) for dx in range(4) for dz in range(4) if dx + dz]
    line_peers = [(m * 2 + o, device(m=m, other=bool(o))) for m in range(4) for o in range(2) if m + o]
    neighbours = [to for _, to in row_peers + col_peers] + [to for k, to in diagonal_peers if k & 2]
    neighbours += [to for k, to in plane_peers if k // 4 and k % 4] + [to for k, to in line_peers if k == 5]
    barrier = pltpu.get_barrier_semaphore()
    for other in neighbours:
        pl.semaphore_signal(barrier, inc=1, device_id=other, device_id_type=MESH)
    pl.semaphore_wait(barrier, len(neighbours))

    def flip(bit, value):
        return 1 - value if bit else value

    def columns(h):
        return pl.ds(pl.multiple_of(h * HALF, HALF), HALF)

    def l_part(s, m, dz=0):
        return lbuf.at[s, flip(m & 1, yl), (z + dz) % 4, flip(m & 2, yh)]

    def r_part(p, m, dx=0):
        return rbuf.at[p, (x + dx) % 4, flip(m, yh)]

    def own_tokens(h):
        return pl.ds(pl.multiple_of(h * TOK, TOK), TOK)

    quarter = pl.ds(pl.multiple_of(dp * 128, 128), 128)
    own_weights = pltpu.make_async_copy(weights.at[:, quarter, :], share, s_share.at[0])
    local = []
    for s in range(2):
        copy = pltpu.make_async_copy(inputs.at[s, own_tokens(yl), :], l_part(s, 0), s_loc.at[s])
        copy.start()
        local.append(copy)
    for p in range(4):
        copy = pltpu.make_async_copy(out_grads.at[p, :, columns(half[p])], r_part(p, 0), s_loc.at[2 + p])
        copy.start()
        local.append(copy)

    ly, ry, xa, xb, xf, zz, zf = {}, {}, {}, {}, {}, {}, {}

    def send_ly(s, m):
        rows = own_tokens(flip(m & 1, yl))
        ly[s, m] = send(inputs.at[s, rows, :], l_part(s, 0), s_ly.at[s, m - 1], r_ly.at[s, m - 1], device(m=m))

    def send_ry(p):
        ry[p] = send(out_grads.at[p, :, columns(1 - half[p])], r_part(p, 0), s_ry.at[p], r_ry.at[p], device(m=2))

    def send_xa(p, ways=(0, 1)):
        for d in ways:
            xa[p, d] = send(out_grads.at[p, :, columns(half[p])], r_part(p, 0), s_xa.at[p, d], r_xa.at[p, d], device(dx=1 - 2 * d))

    def send_xb(p, ways=(0, 1)):
        if not [k for k in xb if k[0] == p]:
            ry[p].wait_recv()
        for d in ways:
            xb[p, d] = send(r_part(p, 1), r_part(p, 1), s_xb.at[p, d], r_xb.at[p, d], device(dx=1 - 2 * d))

    def send_xfa(p):
        xa[p, 0].wait_recv()
        xf[p, 0] = send(r_part(p, 0, -1), r_part(p, 0, -1), s_xf.at[p, 0], r_xf.at[p, 0], device(dx=1))

    def send_xfb(p):
        xb[p, 1].wait_recv()
        xf[p, 1] = send(r_part(p, 1, 1), r_part(p, 1, 1), s_xf.at[p, 1], r_xf.at[p, 1], device(dx=-1))

    def send_z(s, m):
        if m:
            ly[s, m].wait_recv()
        for d in range(2):
            src = l_part(s, m) if m else inputs.at[s, own_tokens(yl), :]
            zz[s, m, d] = send(src, l_part(s, m), s_z.at[s, m, d], r_z.at[s, m, d], device(dz=1 - 2 * d))

    def send_zf(s, m):
        d = m // 2
        back = 2 * d - 1
        zz[s, m, d].wait_recv()
        zf[s, m] = send(l_part(s, m, back), l_part(s, m, back), s_zf.at[s, m], r_zf.at[s, m], device(dz=-back))

    core, pair, to_core, to_y, fwd, outs = {}, {}, {}, {}, {}, []
    mine = pl.ds(pl.multiple_of(c * TOK, TOK), TOK)
    theirs = pl.ds(pl.multiple_of((1 - c) * TOK, TOK), TOK)

    def wait_r(p):
        local[2 + p].wait()
        for d in range(2):
            if d == 1:
                xa[p, d].wait_recv()
            else:
                xb[p, d].wait_recv()
            xf[p, d].wait_recv()

    def wait_l(s):
        local[s].wait()
        for m in range(4):
            zz[s, m, 1 - m // 2].wait_recv()
            zf[s, m].wait_recv()

    def compute(p):
        s = 0 if p < 3 else 1
        right = rbuf[p].reshape(8 * TOK, HALF)

        def rows(l, rs):
            left = lbuf[s, l, :, :, :, rs].reshape(8 * TOK, TOK)
            part[p, l, rs, :] = lax.dot_general(
                left, right, (((0,), (0,)), ((), ())), preferred_element_type=jnp.float32
            )

        to = device(m=3 if p % 2 else 1)
        for k, l in enumerate((1 - yl, yl)):
            rows(l, theirs)
            core[p, k] = send(
                part.at[p, l, theirs, :], core_in.at[p, l], s_core.at[p, k], r_core.at[p, k], device(other=True)
            )
            rows(l, mine)
            core[p, k].wait_recv()
            part[p, l, mine, :] += core_in[p, l]
            if k == 0:
                pair[p] = send(part.at[p, l, mine, :], pair_in.at[p], s_pair.at[p], r_pair.at[p], to)

    def lanes(value):
        return jnp.broadcast_to(value, (1, 128))

    def weight_sums():
        own_weights.wait()
        for p in range(4):
            total = jnp.zeros((8, 1024), jnp.float32)
            for i in range(16):
                block = share[p, 8 * i : 8 * i + 8, :]
                total = total + block * block
            sum1[plane_slot, 2, p : p + 1, :] = lanes(jnp.sum(total))

    def exact_dot(a, b, dims):
        return lax.dot_general(
            a, b, (dims, ((), ())), precision=lax.Precision.HIGHEST, preferred_element_type=jnp.float32
        )

    plane_slot, line_slot = x * 4 + z, dp * 2 + yl
    row_slot, col_slot, dcol_slot = z * 2 + yh, x * 4 + yl * 2 + c, x * 4 + yh * 2 + c

    def statistics(p):
        squares = final[p] * final[p] + 1e-30
        sums = jnp.sum(squares, axis=0, keepdims=True)
        if p % 2:
            dcolx[dcol_slot, p // 2 : p // 2 + 1, :] = sums
        else:
            colx[col_slot, p // 2 : p // 2 + 1, :] = sums
        sums = exact_dot(jnp.ones((8, HALF), jnp.float32), squares, ((1,), (1,)))
        rowx[row_slot, p : p + 1, :] = sums[0:1]

    def exchange(buf, slot, peers, ss, rs):
        return [send(buf.at[slot], buf.at[slot], ss.at[k], rs.at[k], to) for k, to in peers]

    def landed(copies):
        for copy in copies:
            copy.wait_recv()

    def hand_on(p):
        here = out.at[p, mine, columns(half[p])]
        to_y[p] = send(code.at[p], here, s_gy.at[p], r_gy.at[p], device(m=2))
        to_core[p] = send(code.at[p], here, s_gc.at[p], r_gc.at[p], device(other=True))
        copy = pltpu.make_async_copy(code.at[p], here, s_out.at[p])
        copy.start()
        outs.append(copy)

    def finish(p):
        pair[p].wait_recv()
        gradient = part[p, yl, mine, :] + pair_in[p]
        final[p] = gradient
        statistics(p)
        if p == 2:
            stats.append(exchange(colx, col_slot, col_peers, s_cx, r_cx))
        if p == 3:
            stats.append(exchange(rowx, row_slot, row_peers, s_rx, r_rx))
            stats.append(exchange(dcolx, dcol_slot, diagonal_peers, s_dx, r_dx))
        norm = jnp.sum(gradient * gradient + 1e-30, axis=1, keepdims=True)
        code[p] = encode(gradient * (TOP * lax.rsqrt(norm))).astype(jnp.bfloat16)

    def forward(p):
        to_y[p].wait_recv()
        there = out.at[p, mine, columns(1 - half[p])]
        fwd[p] = send(there, there, s_gf.at[p], r_gf.at[p], device(other=True))

    stats = []
    send_ly(0, 1)
    send_ly(0, 3)
    send_xa(0)
    send_z(0, 0)
    send_xa(1)
    own_weights.start()
    send_z(0, 1)
    send_z(0, 3)
    send_ry(0)
    send_ly(0, 2)
    send_ry(1)
    send_xa(2)
    weight_sums()
    send_xb(0)
    send_xfa(0)
    send_z(0, 2)
    send_zf(0, 0)
    send_zf(0, 1)
    send_xfb(0)
    send_ry(2)
    send_xb(1)
    send_zf(0, 3)
    send_zf(0, 2)
    send_xfa(1)
    send_ly(1, 1)
    send_ly(1, 3)
    send_ly(1, 2)
    send_ry(3)
    send_z(1, 0)
    send_xfb(1)
    send_xb(2)
    send_xa(3, (0,))
    send_z(1, 1)
    early = len(sent) - 12
    wait_r(0)
    wait_l(0)
    compute(0)
    send_z(1, 3)
    send_xb(3, (1,))
    send_xfa(2)
    wait_r(1)
    compute(1)
    send_z(1, 2)
    send_xfb(2)
    send_xa(3, (1,))
    send_xb(3, (0,))
    send_zf(1, 0)
    send_zf(1, 1)
    send_zf(1, 3)
    drain(early // 2)
    finish(0)
    hand_on(0)
    send_zf(1, 2)
    send_xfa(3)
    send_xfb(3)
    drain(early)
    finish(1)
    hand_on(1)
    wait_r(2)
    late = len(sent) - 6
    compute(2)
    wait_r(3)
    wait_l(1)
    compute(3)
    drain(late)
    forward(0)
    finish(2)
    hand_on(2)
    finish(3)

    decay = 1.0 - float(STEP) ** (-0.8)
    tail = len(sent)
    landed(stats[1])
    sums = rowx[0]
    for k in range(1, 8):
        sums = sums + rowx[k]
    rows_new = decay * row_moment[:, mine] + (1.0 - decay) * (sums / D)
    rown[c, 0] = rows_new
    for h in range(2):
        rown[c, 1 + h] = rowx[z * 2 + h]
    to_rn = send(rown.at[c], rown.at[c], s_rn.at[0], r_rn.at[0], device(other=True))
    landed(stats[0])
    sums = colx[0]
    for k in range(1, 16):
        sums = sums + colx[k]
    for p in (0, 2):
        old = col_moment[p : p + 1, columns(half[p])]
        coln[yh, p : p + 1, :] = decay * old + (1.0 - decay) * (sums[p // 2 : p // 2 + 1] / D)
    landed(stats[2])
    sums = dcolx[0]
    for k in range(1, 16):
        sums = sums + dcolx[k]
    for p in (1, 3):
        old = col_moment[p : p + 1, columns(half[p])]
        coln[yh, p : p + 1, :] = decay * old + (1.0 - decay) * (sums[p // 2 : p // 2 + 1] / D)
    cols_new = coln[yh]
    to_cn = send(coln.at[yh], coln.at[yh], s_cn.at[0], r_cn.at[0], device(m=2))
    hand_on(3)
    for p in range(4):
        sum1[plane_slot, 0, p : p + 1, :] = lanes(jnp.sum(rows_new[p : p + 1]) * 0.125)
        by_row = jnp.broadcast_to(1.0 / rows_new[p : p + 1], (8, TOK))
        by_col = exact_dot(by_row, final[p] * final[p], ((1,), (0,)))
        sum1[plane_slot, 1, p : p + 1, :] = lanes(jnp.sum(by_col[0:1] / cols_new[p : p + 1]))
    landed(exchange(sum1, plane_slot, plane_peers, s_s1, r_s1))
    sums = sum1[0]
    for k in range(1, 16):
        sums = sums + sum1[k]
    sum2[line_slot] = sums
    lines = exchange(sum2, line_slot, line_peers, s_s2, r_s2)
    drain(tail)
    forward(1)
    forward(2)
    forward(3)
    landed(lines)
    sums = sum2[0]
    for k in range(1, 8):
        sums = sums + sum2[k]
    mean_row = sums[0] / D
    clip = jnp.maximum(1.0, jnp.sqrt(sums[1] * mean_row / (D * D)))
    size = min(0.01, float(STEP) ** (-0.5)) * jnp.maximum(0.001, jnp.sqrt(sums[2] / (D * D)))
    factor = (-(size / clip) * jnp.sqrt(mean_row))[:, 0:1]
    to_rn.wait_recv()
    to_cn.wait_recv()
    for k in range(2):
        out_row[:, TOK * k : TOK * (k + 1)] = rown[k, 0]
        for h in range(2):
            rows_left = factor * lax.rsqrt(rown[k, 0]) * jnp.sqrt(rown[k, 1 + h]) * (1.0 / TOP)
            for p in range(4):
                out_left[p, (h + yl) % 2 if p % 2 else h, :, TOK * k : TOK * (k + 1)] = jnp.broadcast_to(rows_left[p : p + 1], (8, TOK))
        cols_right = lax.rsqrt(coln[k])
        for p in range(4):
            place = columns((k + yl) % 2) if p % 2 else pl.ds(HALF * k, HALF)
            out_col[p : p + 1, place] = coln[k, p : p + 1, :]
            out_right[p, :, place] = cols_right[p : p + 1]

    for p in range(4):
        to_core[p].wait_recv()
        fwd[p].wait_recv()
        outs[p].wait()
    drain(len(sent))


def gradients(inputs, out_grads, weights, row_moment, col_moment):
    dma = pltpu.SemaphoreType.DMA
    any_space = pl.BlockSpec(memory_space=pl.ANY)
    vmem = pl.BlockSpec(memory_space=pltpu.VMEM)
    f32 = jnp.float32
    return pl.pallas_call(
        gradient_kernel,
        out_shape=[
            jax.ShapeDtypeStruct((4, 512, 1024), jnp.bfloat16),
            jax.ShapeDtypeStruct((4, 512), f32),
            jax.ShapeDtypeStruct((4, 1024), f32),
            jax.ShapeDtypeStruct((4, 2, 8, 512), f32),
            jax.ShapeDtypeStruct((4, 1, 1024), f32),
        ],
        in_specs=[any_space, any_space, any_space, vmem, vmem],
        out_specs=[any_space, vmem, vmem, vmem, vmem],
        scratch_shapes=[
            pltpu.VMEM((2, 2, 4, 2, TOK, HALF), jnp.bfloat16),
            pltpu.VMEM((4, 4, 2, TOK, HALF), jnp.bfloat16),
            pltpu.VMEM((4, 2, 512, HALF), f32),
            pltpu.VMEM((4, 2, TOK, HALF), f32),
            pltpu.VMEM((4, TOK, HALF), f32),
            pltpu.VMEM((4, TOK, HALF), f32),
            pltpu.VMEM((4, TOK, HALF), jnp.bfloat16),
            pltpu.VMEM((4, 128, 1024), f32),
            pltpu.VMEM((8, 4, TOK), f32),
            pltpu.VMEM((16, 2, HALF), f32),
            pltpu.VMEM((16, 2, HALF), f32),
            pltpu.VMEM((2, 3, 4, TOK), f32),
            pltpu.VMEM((2, 4, HALF), f32),
            pltpu.VMEM((16, 3, 4, 128), f32),
            pltpu.VMEM((8, 3, 4, 128), f32),
            dma((6,)),
            dma((2, 3)), dma((2, 3)), dma((4,)), dma((4,)),
            dma((4, 2)), dma((4, 2)), dma((4, 2)), dma((4, 2)), dma((4, 2)), dma((4, 2)),
            dma((2, 4, 2)), dma((2, 4, 2)), dma((2, 4)), dma((2, 4)),
            dma((4, 2)), dma((4, 2)), dma((4,)), dma((4,)),
            dma((4,)), dma((4,)), dma((4,)), dma((4,)), dma((4,)), dma((4,)), dma((4,)),
            dma((1,)), dma((8,)), dma((8,)), dma((16,)), dma((16,)), dma((16,)), dma((16,)),
            dma((1,)), dma((1,)), dma((1,)), dma((1,)), dma((16,)), dma((16,)), dma((8,)), dma((8,)),
        ],
        name="gradients",
        compiler_params=pltpu.CompilerParams(
            collective_id=0, has_side_effects=True, vmem_limit_bytes=56 * 2**20
        ),
    )(inputs, out_grads, weights, row_moment, col_moment)


def local(inputs, out_grads, weights, row_moment, col_moment):
    code, row_new, col_new, left, right = gradients(inputs, out_grads, weights, row_moment, col_moment)
    any_space = pl.BlockSpec(memory_space=pl.ANY)
    f32 = jnp.float32
    return pl.pallas_call(
        scale_kernel,
        out_shape=[
            jax.ShapeDtypeStruct((4, 512, 1024), f32),
            jax.ShapeDtypeStruct((4, 512), f32),
            jax.ShapeDtypeStruct((4, 1024), f32),
        ],
        in_specs=[any_space] * 5,
        out_specs=[any_space] * 3,
        scratch_shapes=[
            pltpu.VMEM((4, 512, 1024), jnp.bfloat16),
            pltpu.VMEM((4, 512, 1024), f32),
            pltpu.VMEM((4, 2, 8, 512), f32),
            pltpu.VMEM((4, 1, 1024), f32),
            pltpu.SemaphoreType.DMA((4, 2)),
            pltpu.SemaphoreType.DMA((4, 2)),
            pltpu.SemaphoreType.DMA((4,)),
        ],
        name="scale",
        compiler_params=pltpu.CompilerParams(vmem_limit_bytes=60 * 2**20),
    )(code, left, right, row_new, col_new)


def solution(mesh):
    return jax.shard_map(
        local,
        mesh=mesh,
        in_specs=(
            P(None, ("dp", "col"), "row"),
            P(None, ("dp", "row"), "col"),
            P(None, "row", "col"),
            P(None, "row"),
            P(None, "col"),
        ),
        out_specs=(P(None, "row", "col"), P(None, "row"), P(None, "col")),
        check_vma=False,
    )
```

```python
import jax
import jax.numpy as jnp
from jax import lax
from jax.experimental import pallas as pl
from jax.experimental.pallas import tpu as pltpu
from jax.sharding import PartitionSpec as P

D = 4096
STEP = 10
MESH = pl.DeviceIdType.MESH
TOK = 256
HALF = 512


TOP = 2.0**7.75


def encode(v):
    square = v * v
    fourth = square * square
    eighth = fourth * fourth
    power = eighth * eighth
    return jnp.where(v < 0, -power, power)


def decode(y):
    return y * jnp.exp2(jnp.log2(jnp.maximum(jnp.abs(y), 1e-37)) * (-15.0 / 16.0))


def scale_kernel(
    code, left_in, right_in, row_new, col_new, out, out_row, out_col, codes, changes, left, right, s_in, s_out, s_small
):
    blocks = [(p, i) for p in range(4) for i in range(2)]
    rows = [pl.ds(TOK * i, TOK) for i in range(2)]
    loads = [pltpu.make_async_copy(code.at[p, rows[i]], codes.at[p, rows[i]], s_in.at[p, i]) for p, i in blocks]
    stores = [pltpu.make_async_copy(changes.at[p, rows[i]], out.at[p, rows[i]], s_out.at[p, i]) for p, i in blocks]
    small = [
        pltpu.make_async_copy(a, b, s_small.at[k])
        for k, (a, b) in enumerate([(left_in, left), (right_in, right), (row_new, out_row), (col_new, out_col)])
    ]
    for load in small + loads:
        load.start()
    small[0].wait()
    small[1].wait()
    for k, (p, i) in enumerate(blocks):
        loads[k].wait()
        for h in range(2):
            cols = pl.ds(HALF * h, HALF)
            col = jnp.transpose(left[p, h, :, rows[i]])[:, 0:1]
            changes[p, rows[i], cols] = decode(codes[p, rows[i], cols].astype(jnp.float32)) * (col * right[p, :, cols])
        stores[k].start()
    for store in stores + small[2:]:
        store.wait()


def gradient_kernel(
    inputs, out_grads, weights, row_moment, col_moment, out, out_row, out_col, out_left, out_right,
    lbuf, rbuf, part, core_in, pair_in, final, code, share, rowx, colx, dcolx, rown, coln, sum1, sum2,
    s_loc, s_ly, r_ly, s_ry, r_ry, s_xa, r_xa, s_xb, r_xb, s_xf, r_xf,
    s_z, r_z, s_zf, r_zf, s_core, r_core, s_pair, r_pair, s_gc, r_gc, s_gy, r_gy, s_gf, r_gf, s_out,
    s_share, s_rx, r_rx, s_cx, r_cx, s_dx, r_dx, s_rn, r_rn, s_cn, r_cn, s_s1, r_s1, s_s2, r_s2,
):
    dp, row, z = lax.axis_index("dp"), lax.axis_index("row"), lax.axis_index("col")
    yh, c, x, yl = dp // 2, dp % 2, row // 2, row % 2

    def device(dx=0, m=0, dz=0, other=False):
        h = 1 - yh if m & 2 else yh
        l = 1 - yl if m & 1 else yl
        return {
            "dp": h * 2 + (1 - c if other else c),
            "row": ((x + dx) % 4) * 2 + l,
            "col": (z + dz) % 4,
        }

    def send(src, dst, ss, rs, to):
        copy = pltpu.make_async_remote_copy(
            src_ref=src, dst_ref=dst, send_sem=ss, recv_sem=rs, device_id=to, device_id_type=MESH
        )
        copy.start()
        sent.append(copy)
        return copy

    sent, drained = [], [0]

    def drain(count):
        for copy in sent[drained[0] : count]:
            copy.wait_send()
        drained[0] = max(drained[0], count)

    half = [yh, (yh + yl) % 2, yh, (yh + yl) % 2]
    row_peers = [(dz * 2 + h, device(dz=dz, m=2 * h)) for dz in range(4) for h in range(2) if dz + h]
    col_peers = [
        (dx * 4 + l * 2 + o, device(dx=dx, m=l, other=bool(o)))
        for dx in range(4) for l in range(2) for o in range(2) if dx + l + o
    ]
    diagonal_peers = [
        (dx * 4 + l * 2 + o, device(dx=dx, m=3 * l, other=bool(o)))
        for dx in range(4) for l in range(2) for o in range(2) if dx + l + o
    ]
    plane_peers = [(dx * 4 + dz, device(dx=dx, dz=dz)) for dx in range(4) for dz in range(4) if dx + dz]
    line_peers = [(m * 2 + o, device(m=m, other=bool(o))) for m in range(4) for o in range(2) if m + o]
    neighbours = [to for _, to in row_peers + col_peers] + [to for k, to in diagonal_peers if k & 2]
    neighbours += [to for k, to in plane_peers if k // 4 and k % 4] + [to for k, to in line_peers if k == 5]
    barrier = pltpu.get_barrier_semaphore()
    for other in neighbours:
        pl.semaphore_signal(barrier, inc=1, device_id=other, device_id_type=MESH)
    pl.semaphore_wait(barrier, len(neighbours))

    def flip(bit, value):
        return 1 - value if bit else value

    def columns(h):
        return pl.ds(pl.multiple_of(h * HALF, HALF), HALF)

    def l_part(s, m, dz=0):
        return lbuf.at[s, flip(m & 1, yl), (z + dz) % 4, flip(m & 2, yh)]

    def r_part(p, m, dx=0):
        return rbuf.at[p, (x + dx) % 4, flip(m, yh)]

    def own_tokens(h):
        return pl.ds(pl.multiple_of(h * TOK, TOK), TOK)

    quarter = pl.ds(pl.multiple_of(dp * 128, 128), 128)
    own_weights = pltpu.make_async_copy(weights.at[:, quarter, :], share, s_share.at[0])
    local = []
    for s in range(2):
        copy = pltpu.make_async_copy(inputs.at[s, own_tokens(yl), :], l_part(s, 0), s_loc.at[s])
        copy.start()
        local.append(copy)
    for p in range(4):
        copy = pltpu.make_async_copy(out_grads.at[p, :, columns(half[p])], r_part(p, 0), s_loc.at[2 + p])
        copy.start()
        local.append(copy)

    ly, ry, xa, xb, xf, zz, zf = {}, {}, {}, {}, {}, {}, {}

    def send_ly(s, m):
        rows = own_tokens(flip(m & 1, yl))
        ly[s, m] = send(inputs.at[s, rows, :], l_part(s, 0), s_ly.at[s, m - 1], r_ly.at[s, m - 1], device(m=m))

    def send_ry(p):
        ry[p] = send(out_grads.at[p, :, columns(1 - half[p])], r_part(p, 0), s_ry.at[p], r_ry.at[p], device(m=2))

    def send_xa(p, ways=(0, 1)):
        for d in ways:
            xa[p, d] = send(out_grads.at[p, :, columns(half[p])], r_part(p, 0), s_xa.at[p, d], r_xa.at[p, d], device(dx=1 - 2 * d))

    def send_xb(p, ways=(0, 1)):
        if not [k for k in xb if k[0] == p]:
            ry[p].wait_recv()
        for d in ways:
            xb[p, d] = send(r_part(p, 1), r_part(p, 1), s_xb.at[p, d], r_xb.at[p, d], device(dx=1 - 2 * d))

    def send_xfa(p):
        xa[p, 0].wait_recv()
        xf[p, 0] = send(r_part(p, 0, -1), r_part(p, 0, -1), s_xf.at[p, 0], r_xf.at[p, 0], device(dx=1))

    def send_xfb(p):
        xb[p, 1].wait_recv()
        xf[p, 1] = send(r_part(p, 1, 1), r_part(p, 1, 1), s_xf.at[p, 1], r_xf.at[p, 1], device(dx=-1))

    def send_z(s, m):
        if m:
            ly[s, m].wait_recv()
        for d in range(2):
            src = l_part(s, m) if m else inputs.at[s, own_tokens(yl), :]
            zz[s, m, d] = send(src, l_part(s, m), s_z.at[s, m, d], r_z.at[s, m, d], device(dz=1 - 2 * d))

    def send_zf(s, m):
        d = m // 2
        back = 2 * d - 1
        zz[s, m, d].wait_recv()
        zf[s, m] = send(l_part(s, m, back), l_part(s, m, back), s_zf.at[s, m], r_zf.at[s, m], device(dz=-back))

    core, pair, to_core, to_y, fwd, outs = {}, {}, {}, {}, {}, []
    mine = pl.ds(pl.multiple_of(c * TOK, TOK), TOK)
    theirs = pl.ds(pl.multiple_of((1 - c) * TOK, TOK), TOK)

    def wait_r(p):
        local[2 + p].wait()
        for d in range(2):
            if d == 1:
                xa[p, d].wait_recv()
            else:
                xb[p, d].wait_recv()
            xf[p, d].wait_recv()

    def wait_l(s):
        local[s].wait()
        for m in range(4):
            zz[s, m, 1 - m // 2].wait_recv()
            zf[s, m].wait_recv()

    def compute(p):
        s = 0 if p < 3 else 1
        right = rbuf[p].reshape(8 * TOK, HALF)

        def rows(l, rs):
            left = lbuf[s, l, :, :, :, rs].reshape(8 * TOK, TOK)
            part[p, l, rs, :] = lax.dot_general(
                left, right, (((0,), (0,)), ((), ())), preferred_element_type=jnp.float32
            )

        to = device(m=3 if p % 2 else 1)
        for k, l in enumerate((1 - yl, yl)):
            rows(l, theirs)
            core[p, k] = send(
                part.at[p, l, theirs, :], core_in.at[p, l], s_core.at[p, k], r_core.at[p, k], device(other=True)
            )
            rows(l, mine)
            core[p, k].wait_recv()
            part[p, l, mine, :] += core_in[p, l]
            if k == 0:
                pair[p] = send(part.at[p, l, mine, :], pair_in.at[p], s_pair.at[p], r_pair.at[p], to)

    def lanes(value):
        return jnp.broadcast_to(value, (1, 128))

    def weight_sums():
        own_weights.wait()
        for p in range(4):
            total = jnp.zeros((8, 1024), jnp.float32)
            for i in range(16):
                block = share[p, 8 * i : 8 * i + 8, :]
                total = total + block * block
            sum1[plane_slot, 2, p : p + 1, :] = lanes(jnp.sum(total))

    def exact_dot(a, b, dims):
        return lax.dot_general(
            a, b, (dims, ((), ())), precision=lax.Precision.HIGHEST, preferred_element_type=jnp.float32
        )

    plane_slot, line_slot = x * 4 + z, dp * 2 + yl
    row_slot, col_slot, dcol_slot = z * 2 + yh, x * 4 + yl * 2 + c, x * 4 + yh * 2 + c

    def statistics(p):
        squares = final[p] * final[p] + 1e-30
        sums = jnp.sum(squares, axis=0, keepdims=True)
        if p % 2:
            dcolx[dcol_slot, p // 2 : p // 2 + 1, :] = sums
        else:
            colx[col_slot, p // 2 : p // 2 + 1, :] = sums
        sums = exact_dot(jnp.ones((8, HALF), jnp.float32), squares, ((1,), (1,)))
        rowx[row_slot, p : p + 1, :] = sums[0:1]

    def exchange(buf, slot, peers, ss, rs):
        return [send(buf.at[slot], buf.at[slot], ss.at[k], rs.at[k], to) for k, to in peers]

    def landed(copies):
        for copy in copies:
            copy.wait_recv()

    def hand_on(p):
        here = out.at[p, mine, columns(half[p])]
        to_y[p] = send(code.at[p], here, s_gy.at[p], r_gy.at[p], device(m=2))
        to_core[p] = send(code.at[p], here, s_gc.at[p], r_gc.at[p], device(other=True))
        copy = pltpu.make_async_copy(code.at[p], here, s_out.at[p])
        copy.start()
        outs.append(copy)

    def finish(p):
        pair[p].wait_recv()
        gradient = part[p, yl, mine, :] + pair_in[p]
        final[p] = gradient
        norm = jnp.sum(gradient * gradient + 1e-30, axis=1, keepdims=True)
        code[p] = encode(gradient * (TOP * lax.rsqrt(norm))).astype(jnp.bfloat16)
        if p < 3:
            hand_on(p)
        statistics(p)
        if p == 2:
            stats.append(exchange(colx, col_slot, col_peers, s_cx, r_cx))
        if p == 3:
            stats.append(exchange(rowx, row_slot, row_peers, s_rx, r_rx))
            stats.append(exchange(dcolx, dcol_slot, diagonal_peers, s_dx, r_dx))

    def forward(p):
        to_y[p].wait_recv()
        there = out.at[p, mine, columns(1 - half[p])]
        fwd[p] = send(there, there, s_gf.at[p], r_gf.at[p], device(other=True))

    stats = []
    send_ly(0, 1)
    send_ly(0, 3)
    send_xa(0)
    send_z(0, 0)
    send_xa(1)
    own_weights.start()
    send_z(0, 1)
    send_z(0, 3)
    send_ry(0)
    send_ly(0, 2)
    send_ry(1)
    send_ry(2)
    send_xa(2)
    weight_sums()
    send_xb(0)
    send_xfa(0)
    send_z(0, 2)
    send_zf(0, 0)
    send_zf(0, 1)
    send_ly(1, 1)
    send_ly(1, 3)
    send_ly(1, 2)
    send_ry(3)
    send_xfb(0)
    send_xb(1)
    send_zf(0, 3)
    send_zf(0, 2)
    send_xfa(1)
    send_z(1, 0)
    send_xfb(1)
    send_xb(2)
    send_xa(3, (0,))
    send_z(1, 1)
    early = len(sent) - 12
    wait_r(0)
    wait_l(0)
    compute(0)
    send_z(1, 3)
    send_xb(3, (1,))
    send_xfa(2)
    wait_r(1)
    compute(1)
    send_z(1, 2)
    send_xfb(2)
    send_xa(3, (1,))
    send_xb(3, (0,))
    send_zf(1, 0)
    send_zf(1, 1)
    send_zf(1, 3)
    drain(early // 2)
    finish(0)
    send_zf(1, 2)
    send_xfa(3)
    send_xfb(3)
    drain(early)
    finish(1)
    wait_r(2)
    late = len(sent) - 6
    compute(2)
    wait_r(3)
    wait_l(1)
    compute(3)
    drain(late)
    forward(0)
    finish(2)
    finish(3)

    decay = 1.0 - float(STEP) ** (-0.8)
    tail = len(sent)
    landed(stats[1])
    sums = rowx[0]
    for k in range(1, 8):
        sums = sums + rowx[k]
    rows_new = decay * row_moment[:, mine] + (1.0 - decay) * (sums / D)
    rown[c, 0] = rows_new
    for h in range(2):
        rown[c, 1 + h] = rowx[z * 2 + h]
    to_rn = send(rown.at[c], rown.at[c], s_rn.at[0], r_rn.at[0], device(other=True))
    landed(stats[0])
    sums = colx[0]
    for k in range(1, 16):
        sums = sums + colx[k]
    for p in (0, 2):
        old = col_moment[p : p + 1, columns(half[p])]
        coln[yh, p : p + 1, :] = decay * old + (1.0 - decay) * (sums[p // 2 : p // 2 + 1] / D)
    landed(stats[2])
    hand_on(3)
    sums = dcolx[0]
    for k in range(1, 16):
        sums = sums + dcolx[k]
    for p in (1, 3):
        old = col_moment[p : p + 1, columns(half[p])]
        coln[yh, p : p + 1, :] = decay * old + (1.0 - decay) * (sums[p // 2 : p // 2 + 1] / D)
    cols_new = coln[yh]
    to_cn = send(coln.at[yh], coln.at[yh], s_cn.at[0], r_cn.at[0], device(m=2))
    for p in range(4):
        sum1[plane_slot, 0, p : p + 1, :] = lanes(jnp.sum(rows_new[p : p + 1]) * 0.125)
        by_row = jnp.broadcast_to(1.0 / rows_new[p : p + 1], (8, TOK))
        by_col = exact_dot(by_row, final[p] * final[p], ((1,), (0,)))
        sum1[plane_slot, 1, p : p + 1, :] = lanes(jnp.sum(by_col[0:1] / cols_new[p : p + 1]))
    landed(exchange(sum1, plane_slot, plane_peers, s_s1, r_s1))
    sums = sum1[0]
    for k in range(1, 16):
        sums = sums + sum1[k]
    sum2[line_slot] = sums
    lines = exchange(sum2, line_slot, line_peers, s_s2, r_s2)
    drain(tail)
    forward(1)
    forward(2)
    forward(3)
    landed(lines)
    sums = sum2[0]
    for k in range(1, 8):
        sums = sums + sum2[k]
    mean_row = sums[0] / D
    clip = jnp.maximum(1.0, jnp.sqrt(sums[1] * mean_row / (D * D)))
    size = min(0.01, float(STEP) ** (-0.5)) * jnp.maximum(0.001, jnp.sqrt(sums[2] / (D * D)))
    factor = (-(size / clip) * jnp.sqrt(mean_row))[:, 0:1]
    to_rn.wait_recv()
    to_cn.wait_recv()
    for k in range(2):
        out_row[:, TOK * k : TOK * (k + 1)] = rown[k, 0]
        for h in range(2):
            rows_left = factor * lax.rsqrt(rown[k, 0]) * jnp.sqrt(rown[k, 1 + h]) * (1.0 / TOP)
            for p in range(4):
                out_left[p, (h + yl) % 2 if p % 2 else h, :, TOK * k : TOK * (k + 1)] = jnp.broadcast_to(rows_left[p : p + 1], (8, TOK))
        cols_right = lax.rsqrt(coln[k])
        for p in range(4):
            place = columns((k + yl) % 2) if p % 2 else pl.ds(HALF * k, HALF)
            out_col[p : p + 1, place] = coln[k, p : p + 1, :]
            out_right[p, :, place] = cols_right[p : p + 1]

    for p in range(4):
        to_core[p].wait_recv()
        fwd[p].wait_recv()
        outs[p].wait()
    drain(len(sent))


def gradients(inputs, out_grads, weights, row_moment, col_moment):
    dma = pltpu.SemaphoreType.DMA
    any_space = pl.BlockSpec(memory_space=pl.ANY)
    vmem = pl.BlockSpec(memory_space=pltpu.VMEM)
    f32 = jnp.float32
    return pl.pallas_call(
        gradient_kernel,
        out_shape=[
            jax.ShapeDtypeStruct((4, 512, 1024), jnp.bfloat16),
            jax.ShapeDtypeStruct((4, 512), f32),
            jax.ShapeDtypeStruct((4, 1024), f32),
            jax.ShapeDtypeStruct((4, 2, 8, 512), f32),
            jax.ShapeDtypeStruct((4, 1, 1024), f32),
        ],
        in_specs=[any_space, any_space, any_space, vmem, vmem],
        out_specs=[any_space, vmem, vmem, vmem, vmem],
        scratch_shapes=[
            pltpu.VMEM((2, 2, 4, 2, TOK, HALF), jnp.bfloat16),
            pltpu.VMEM((4, 4, 2, TOK, HALF), jnp.bfloat16),
            pltpu.VMEM((4, 2, 512, HALF), f32),
            pltpu.VMEM((4, 2, TOK, HALF), f32),
            pltpu.VMEM((4, TOK, HALF), f32),
            pltpu.VMEM((4, TOK, HALF), f32),
            pltpu.VMEM((4, TOK, HALF), jnp.bfloat16),
            pltpu.VMEM((4, 128, 1024), f32),
            pltpu.VMEM((8, 4, TOK), f32),
            pltpu.VMEM((16, 2, HALF), f32),
            pltpu.VMEM((16, 2, HALF), f32),
            pltpu.VMEM((2, 3, 4, TOK), f32),
            pltpu.VMEM((2, 4, HALF), f32),
            pltpu.VMEM((16, 3, 4, 128), f32),
            pltpu.VMEM((8, 3, 4, 128), f32),
            dma((6,)),
            dma((2, 3)), dma((2, 3)), dma((4,)), dma((4,)),
            dma((4, 2)), dma((4, 2)), dma((4, 2)), dma((4, 2)), dma((4, 2)), dma((4, 2)),
            dma((2, 4, 2)), dma((2, 4, 2)), dma((2, 4)), dma((2, 4)),
            dma((4, 2)), dma((4, 2)), dma((4,)), dma((4,)),
            dma((4,)), dma((4,)), dma((4,)), dma((4,)), dma((4,)), dma((4,)), dma((4,)),
            dma((1,)), dma((8,)), dma((8,)), dma((16,)), dma((16,)), dma((16,)), dma((16,)),
            dma((1,)), dma((1,)), dma((1,)), dma((1,)), dma((16,)), dma((16,)), dma((8,)), dma((8,)),
        ],
        name="gradients",
        compiler_params=pltpu.CompilerParams(
            collective_id=0, has_side_effects=True, vmem_limit_bytes=56 * 2**20
        ),
    )(inputs, out_grads, weights, row_moment, col_moment)


def local(inputs, out_grads, weights, row_moment, col_moment):
    code, row_new, col_new, left, right = gradients(inputs, out_grads, weights, row_moment, col_moment)
    any_space = pl.BlockSpec(memory_space=pl.ANY)
    f32 = jnp.float32
    return pl.pallas_call(
        scale_kernel,
        out_shape=[
            jax.ShapeDtypeStruct((4, 512, 1024), f32),
            jax.ShapeDtypeStruct((4, 512), f32),
            jax.ShapeDtypeStruct((4, 1024), f32),
        ],
        in_specs=[any_space] * 5,
        out_specs=[any_space] * 3,
        scratch_shapes=[
            pltpu.VMEM((4, 512, 1024), jnp.bfloat16),
            pltpu.VMEM((4, 512, 1024), f32),
            pltpu.VMEM((4, 2, 8, 512), f32),
            pltpu.VMEM((4, 1, 1024), f32),
            pltpu.SemaphoreType.DMA((4, 2)),
            pltpu.SemaphoreType.DMA((4, 2)),
            pltpu.SemaphoreType.DMA((4,)),
        ],
        name="scale",
        compiler_params=pltpu.CompilerParams(vmem_limit_bytes=60 * 2**20),
    )(code, left, right, row_new, col_new)


def solution(mesh):
    return jax.shard_map(
        local,
        mesh=mesh,
        in_specs=(
            P(None, ("dp", "col"), "row"),
            P(None, ("dp", "row"), "col"),
            P(None, "row", "col"),
            P(None, "row"),
            P(None, "col"),
        ),
        out_specs=(P(None, "row", "col"), P(None, "row"), P(None, "col")),
        check_vma=False,
    )
```
